32 devices in a mesh: ctx: 16 (over z, y, x), fsdp: 2 (over core).
Axes of the slice: x: 2, y: 2, z: 4, core: 2. Of those that a mesh axis runs over, the one named last changes fastest.
Arguments:
- proj: bfloat16 [2, 2048, 12288], P('fsdp', 'ctx'), may hold values from -6 to 6
- short_taps: float32 [7, 12288], P(None, 'fsdp'), may hold values from -2 to 2
- long_filter: float32 [128, 256], P(None, 'fsdp'), may hold values from -0.5 to 0.5
- skip: float32 [4096], P('fsdp'), may hold values from -3 to 3
- grad_out: bfloat16 [2, 2048, 4096], P('fsdp', 'ctx'), may hold values from -6 to 6
- starts: int32 [2, 16, 4], P('fsdp', 'ctx'), may hold values from 0 to 128, as said below
Outputs:
- mixed_out: bfloat16 [2, 2048, 4096], P('fsdp', 'ctx')
- grad_proj: bfloat16 [2, 2048, 12288], P('fsdp', 'ctx')
- grad_short: float32 [7, 12288], P(None, 'fsdp')
- grad_long: float32 [128, 256], P(None, 'fsdp')
- grad_skip: float32 [4096], P('fsdp')
The draws below stay inside these ranges and needn't reach their ends.
Inputs may be any that keep to these rules, and one draw needn't show every extreme that they name: Each list holds positions, within one device's 128 positions, at which documents start, increasing and without repeats; entries equal to 128 are empty and come after all others. Every window's first position starts a document.
All inputs are finite; a program needn't handle non-finite values.
Results may differ from the reference program's by a relative error of at most 0.007.
Values may be sent and summed in bfloat16 or wider, within the bound.
A program may use at most 128 MiB of HBM per device.

```python
import jax
import jax.numpy as jnp
from jax import lax

C = 4096
GROUP = 16
LEN = 128
SHORT = 7
NB = 4
TOK_DEV = 128
GROUPS = 256
SHARDS = 16
WINDOWS = 2
SEQ = 2048


def draw_starts(key, part):
    key = jax.random.fold_in(key, 7)
    order_key, count_key, emptied_key = jax.random.split(key, 3)
    scores = jax.random.randint(order_key, (WINDOWS, SHARDS, TOK_DEV), 0, 1 << 20) * TOK_DEV
    scores = scores + jnp.arange(TOK_DEV, dtype=jnp.int32)
    picked = jnp.sort(jnp.argsort(scores, axis=-1)[..., :NB].astype(jnp.int32), axis=-1)
    picked = picked.at[:, 0, 0].set(0)
    counts = jax.random.randint(count_key, (WINDOWS, SHARDS), 0, NB + 1)
    counts = counts.at[:, 0].set(jnp.maximum(counts[:, 0], 1))
    emptied = jax.random.randint(emptied_key, (WINDOWS, 1), 1, SHARDS)
    counts = jnp.where(jnp.arange(SHARDS, dtype=jnp.int32)[None, :] == emptied, 0, counts)
    slots = jnp.arange(NB, dtype=jnp.int32)
    return jnp.where(slots[None, None, :] < counts[..., None], picked, TOK_DEV).astype(jnp.int32)


def block_levels(key, extent, cuts, smallest, largest):
    gain, own = 1.0, jax.random.fold_in(key, 6)
    for position, parts in cuts:
        heights = jnp.exp(jax.random.uniform(jax.random.fold_in(own, position), (parts,), jnp.float32, smallest / len(cuts), largest / len(cuts)))
        gain = gain * jnp.repeat(heights, extent[position] // parts).reshape([-1 if axis == position else 1 for axis in range(len(extent))])
    return gain


def noise(own_key, extent, spread, bound, shards=(), kind=jnp.bfloat16):
    values = jax.random.normal(own_key, extent, jnp.float32) * spread
    if len(shards) > 0:
        values = block_levels(own_key, extent, shards, -0.22, 0.18) * values
    return jnp.clip(values, min=-bound, max=bound).astype(kind)


def setup_inputs(seed: int = 0) -> dict:
    arg_keys = jax.random.split(jax.random.key(seed), 7)
    proj = noise(arg_keys[0], (WINDOWS, SEQ, 3 * C), 1.0, 6.0, ((0, 2), (1, 16)))
    short_taps = noise(arg_keys[1], (SHORT, 3 * C), SHORT ** -0.5, 2.0, ((1, 2),), jnp.float32)
    long_filter = noise(arg_keys[2], (LEN, GROUPS), LEN ** -0.5, 0.5, ((1, 2),), jnp.float32)
    skip = noise(arg_keys[3], (C,), 1.0, 3.0, ((0, 2),), jnp.float32)
    grad_out = noise(arg_keys[4], (WINDOWS, SEQ, C), 1.0, 6.0, ((0, 2), (1, 16)))
    starts = draw_starts(jax.random.fold_in(arg_keys[6], 71), 0)
    return dict(proj=proj, short_taps=short_taps, long_filter=long_filter, skip=skip, grad_out=grad_out, starts=starts)


def rounded(values):
    return lax.optimization_barrier(values.astype(jnp.bfloat16)).astype(jnp.float32)


def last_starts(starts_w):
    offsets = (jnp.arange(SHARDS, dtype=jnp.int32) * TOK_DEV)[:, None]
    marked = jnp.where(starts_w < TOK_DEV, starts_w + offsets, -1).reshape(-1)
    places = jnp.arange(SEQ, dtype=jnp.int32)
    is_start = jnp.any(marked[:, None] == places[None, :], axis=0)
    return lax.cummax(jnp.where(is_start, places, -1), axis=0)


def band_rows(filt_rows, rows_count, cols_count, lag_base):
    lag_table = jnp.arange(rows_count, dtype=jnp.int32)[:, None] - jnp.arange(cols_count, dtype=jnp.int32)[None, :] + lag_base
    inside = (lag_table >= 0) & (lag_table < LEN)
    picked = filt_rows[:, jnp.clip(lag_table, 0, LEN - 1)]
    return jnp.where(inside[None], picked, 0.0)


def lag_totals(product, rows_count, cols_count):
    groups = product.shape[0]
    flattened = product.reshape(groups, rows_count * cols_count)
    flattened = jnp.concatenate([flattened, jnp.zeros((groups, rows_count), product.dtype)], axis=1)
    totals = jnp.sum(flattened.reshape(groups, rows_count, cols_count + 1), axis=1)
    return totals[:, LEN:0:-1]


def reference(proj, short_taps, long_filter, skip, grad_out, starts):
    filt_rows = rounded(long_filter).T
    win_rows = TOK_DEV + LEN
    ahead = band_rows(filt_rows, TOK_DEV, win_rows, LEN)
    behind = band_rows(filt_rows, win_rows, TOK_DEV, 0)
    places = jnp.arange(SEQ, dtype=jnp.int32)
    local_rows = jnp.arange(TOK_DEV, dtype=jnp.int32)
    window_rows = jnp.arange(win_rows, dtype=jnp.int32)
    blocks = jnp.arange(SHARDS, dtype=jnp.int32)
    highest = lax.Precision.HIGHEST

    def one_window(pieces):
        proj_w, grad_w, starts_w = pieces
        latest = last_starts(starts_w)
        source = proj_w.astype(jnp.float32)
        featured = jnp.zeros((SEQ, 3 * C), jnp.float32)
        for offset in range(SHORT):
            shifted = jnp.concatenate([jnp.zeros((offset, 3 * C), jnp.float32), source[:SEQ - offset]], axis=0)
            featured = featured + short_taps[offset] * jnp.where((latest <= places - offset)[:, None], shifted, 0.0)
        query_feat = featured[:, :C]
        key_feat = featured[:, C:2 * C]
        value_feat = featured[:, 2 * C:]
        gating = rounded(key_feat * value_feat)
        gate_pad = jnp.concatenate([jnp.zeros((LEN, C), jnp.float32), gating], axis=0)

        def ahead_linked(first_row):
            own_latest = lax.dynamic_slice_in_dim(latest, first_row, TOK_DEV, 0)
            return own_latest[:, None] <= (first_row - LEN + window_rows)[None, :]

        def forward_block(block_id):
            first_row = block_id * TOK_DEV
            window = lax.dynamic_slice_in_dim(gate_pad, first_row, win_rows, 0).reshape(win_rows, GROUPS, GROUP)
            weights = jnp.where(ahead_linked(first_row)[None], ahead, 0.0)
            return jnp.einsum("gts,sgc->tgc", weights, window, precision=highest).reshape(TOK_DEV, C)

        long_out = lax.map(forward_block, blocks).reshape(SEQ, C)
        combined = long_out + skip * gating
        mixed_w = (query_feat * combined).astype(jnp.bfloat16)
        upstream = grad_w.astype(jnp.float32)
        grad_query = upstream * combined
        through = upstream * query_feat
        grad_long_in = rounded(through)
        grad_pad = jnp.concatenate([grad_long_in, jnp.zeros((LEN, C), jnp.float32)], axis=0)
        latest_pad = jnp.concatenate([latest, jnp.full((LEN,), SEQ, jnp.int32)])

        def backward_block(block_id):
            first_row = block_id * TOK_DEV
            sources = lax.dynamic_slice_in_dim(grad_pad, first_row, win_rows, 0).reshape(win_rows, GROUPS, GROUP)
            their = lax.dynamic_slice_in_dim(latest_pad, first_row, win_rows, 0)
            linked = their[:, None] <= (first_row + local_rows)[None, :]
            weights = jnp.where(linked[None], behind, 0.0)
            block_grad = jnp.einsum("gut,ugc->tgc", weights, sources, precision=highest).reshape(TOK_DEV, C)
            window = lax.dynamic_slice_in_dim(gate_pad, first_row, win_rows, 0).reshape(win_rows, GROUPS, GROUP)
            rows_blk = lax.dynamic_slice_in_dim(grad_long_in, first_row, TOK_DEV, 0).reshape(TOK_DEV, GROUPS, GROUP)
            product = jnp.einsum("tgc,sgc->gts", rows_blk, window, precision=highest)
            product = jnp.where(ahead_linked(first_row)[None], product, 0.0)
            return block_grad, lag_totals(product, TOK_DEV, win_rows)

        gate_parts, lag_parts = lax.map(backward_block, blocks)
        grad_gate = gate_parts.reshape(SEQ, C) + skip * through
        grad_feat = jnp.concatenate([grad_query, grad_gate * value_feat, grad_gate * key_feat], axis=1)
        feat_pad = jnp.concatenate([grad_feat, jnp.zeros((SHORT, 3 * C), jnp.float32)], axis=0)
        latest_short = jnp.concatenate([latest, jnp.full((SHORT,), SEQ, jnp.int32)])
        grad_source = jnp.zeros((SEQ, 3 * C), jnp.float32)
        short_parts = []
        for offset in range(SHORT):
            later = feat_pad[offset:offset + SEQ]
            their = latest_short[offset:offset + SEQ]
            grad_source = grad_source + short_taps[offset] * jnp.where((their <= places)[:, None], later, 0.0)
            earlier = jnp.concatenate([jnp.zeros((offset, 3 * C), jnp.float32), source[:SEQ - offset]], axis=0)
            earlier = jnp.where((latest <= places - offset)[:, None], earlier, 0.0)
            short_parts.append(jnp.sum(grad_feat * earlier, axis=0))
        return (mixed_w, grad_source.astype(jnp.bfloat16), jnp.stack(short_parts),
                jnp.sum(lag_parts, axis=0).T, jnp.sum(through * gating, axis=0))

    outputs = lax.map(one_window, (proj, grad_out, starts))
    scaling = float(WINDOWS * SEQ) ** -0.5
    return (outputs[0], outputs[1], jnp.sum(outputs[2], axis=0) * scaling,
            jnp.sum(outputs[3], axis=0) * scaling, jnp.sum(outputs[4], axis=0) * scaling)
```

```python
import functools

import jax
import jax.numpy as jnp
from jax import lax
from jax.experimental import pallas as pl
from jax.experimental.pallas import tpu as pltpu
from jax.sharding import PartitionSpec as P

GROUP = 16
LEN = 128
SHORT = 7
LANES = 128
FAR = 1 << 29
MESH = pl.DeviceIdType.MESH


def passed_along(block, axis, distance):
    devices = range(lax.axis_size(axis))
    route = [(i - distance, i) for i in devices if i - distance in devices]
    return lax.ppermute(block, axis, route)


def links(last):
    rows = lax.broadcasted_iota(jnp.int32, (last.shape[0], 1), 0)
    return [last <= rows - offset for offset in range(SHORT)]


def shifted_rows(tail, cur):
    whole = jnp.concatenate([tail[8:16].astype(jnp.float32), cur.astype(jnp.float32)], axis=0)
    return [
        (pltpu.roll(whole, offset, 0) if offset else whole)[8:] for offset in range(SHORT)
    ]


def featurize_kernel(last, q, k, v, qt, kt, vt, qw, kw, vw, up, qf, kf, vf, gate, glin):
    linked = links(last[...])

    def feature(cur, tail, taps):
        total = None
        for offset, rows in enumerate(shifted_rows(tail[...], cur[...])):
            term = taps[offset : offset + 1, :] * jnp.where(linked[offset], rows, 0.0)
            total = term if total is None else total + term
        return total

    query = feature(q, qt, qw)
    qf[...] = query
    key = feature(k, kt, kw)
    kf[...] = key
    value = feature(v, vt, vw)
    vf[...] = value
    gate[...] = (key * value).astype(jnp.bfloat16)
    glin[...] = (up[...].astype(jnp.float32) * query).astype(jnp.bfloat16)


def featurize(last, source, tail, taps, upstream):
    tok, channels = upstream.shape
    width = min(512, channels)
    steps = channels // width

    def part(rows, p):
        return pl.BlockSpec((rows, width), lambda i: (0, i + p * steps))

    own = pl.BlockSpec((tok, width), lambda i: (0, i))
    f32 = jax.ShapeDtypeStruct((tok, channels), jnp.float32)
    half = jax.ShapeDtypeStruct((tok, channels), jnp.bfloat16)
    return pl.pallas_call(
        featurize_kernel,
        grid=(steps,),
        in_specs=[pl.BlockSpec((tok, 1), lambda i: (0, 0))]
        + [part(tok, p) for p in range(3)]
        + [part(16, p) for p in range(3)]
        + [part(SHORT, p) for p in range(3)]
        + [own],
        out_specs=[own] * 5,
        out_shape=[f32, f32, f32, half, half],
        compiler_params=pltpu.CompilerParams(vmem_limit_bytes=40 << 20),
        name="featurize",
    )(last, source, source, source, tail, tail, tail, taps, taps, taps, upstream)


def conv_kernel(
    steps, last, last_row, skip, ahead, behind, gate, gate_prev, glin, glin_next,
    qf, kf, vf, up, q, k, v, qt, kt, vt, qw, kw, vw,
    mixed, grads, low, edge, short, skip_out, lag,
):
    step = pl.program_id(0)
    tok = gate.shape[0]
    win = 2 * tok
    linked = links(last[...])
    cols = lax.broadcasted_iota(jnp.int32, (tok, win), 1)
    rows = lax.broadcasted_iota(jnp.int32, (tok, win), 0)
    ahead_ok = last[...] <= cols - tok
    behind_ok = last_row[...] <= rows
    flip_r = lax.broadcasted_iota(jnp.int32, (tok, tok), 0)
    flip_c = lax.broadcasted_iota(jnp.int32, (tok, tok), 1)
    flip = (flip_r + flip_c == tok - 1).astype(jnp.bfloat16)
    own_gate, own_glin = gate[...], glin[...]
    gate_win = jnp.concatenate([gate_prev[...], own_gate], axis=0)
    glin_win = jnp.concatenate([own_glin, glin_next[...]], axis=0)
    glin_flip = jnp.dot(flip, own_glin, preferred_element_type=jnp.float32)
    flipped = ahead_flipped(last_row, tok)
    lane = lax.broadcasted_iota(jnp.int32, (tok, LANES), 1) // GROUP
    long_out = jnp.zeros((tok, LANES), jnp.float32)
    spread = jnp.zeros((tok, LANES), jnp.float32)
    for g in range(LANES // GROUP):
        mine = lane == g
        tile = jnp.broadcast_to(ahead[g : g + 1, :], (tok, win))
        tile = pltpu.roll(tile, 1, 1, stride=1, stride_axis=0)
        tile = jnp.where(ahead_ok, tile, 0.0).astype(jnp.bfloat16)
        out = jnp.dot(tile, gate_win, preferred_element_type=jnp.float32)
        long_out = jnp.where(mine, out, long_out)
        tile = jnp.broadcast_to(behind[g : g + 1, :], (tok, win))
        tile = pltpu.roll(tile, 0, 1, stride=1, stride_axis=0)
        tile = jnp.where(behind_ok, tile, 0.0).astype(jnp.bfloat16)
        out = jnp.dot(tile, glin_win, preferred_element_type=jnp.float32)
        spread = jnp.where(mine, out, spread)
        picked = jnp.where(mine, glin_flip, 0.0).astype(jnp.bfloat16)
        product = lax.dot_general(
            picked, gate_win, (((1,), (1,)), ((), ())), preferred_element_type=jnp.float32
        )
        product = jnp.where(flipped, product, 0.0)
        product = pltpu.roll(product, tok, 1, stride=1, stride_axis=0)
        lag[g : g + 1, :] = jnp.sum(product, axis=0, keepdims=True)[:, :LEN]
    gate_f = own_gate.astype(jnp.float32)
    query, key, value = qf[...], kf[...], vf[...]
    upstream = up[...].astype(jnp.float32)
    factor = skip[...]
    combined = long_out + factor * gate_f
    mixed[...] = (query * combined).astype(jnp.bfloat16)
    through = upstream * query
    skip_out[...] = jnp.sum(through * gate_f, axis=0, keepdims=True)
    grad_gate = spread + factor * through
    feats = (upstream * combined, grad_gate * value, grad_gate * key)
    for part, (grad, cur, tail, taps) in enumerate(
        zip(feats, (q, k, v), (qt, kt, vt), (qw, kw, vw))
    ):
        total = None
        at = pl.ds(pl.multiple_of((part * steps + step) * LANES, LANES), LANES)
        for offset, earlier in enumerate(shifted_rows(tail[...], cur[...])):
            kept = jnp.where(linked[offset], grad, 0.0)
            short[offset : offset + 1, at] = jnp.sum(kept * earlier, axis=0, keepdims=True)
            moved = jnp.concatenate(
                [jnp.zeros((8, LANES), jnp.float32), taps[offset : offset + 1, :] * kept], axis=0
            )
            if offset:
                moved = pltpu.roll(moved, tok + 8 - offset, 0)
            total = moved if total is None else total + moved
        grads[:, at] = total[8:].astype(jnp.bfloat16)
        low[:, at] = total[tok:]
        edge[:, at] = total[:8]


def ahead_flipped(last_row, tok):
    r = lax.broadcasted_iota(jnp.int32, (tok, tok), 0)
    c = lax.broadcasted_iota(jnp.int32, (tok, tok), 1)
    own = jnp.broadcast_to(last_row[:, :tok], (tok, tok))
    turned = jnp.sum(
        jnp.where(r + c == tok - 1, own, 0).astype(jnp.float32), axis=1, keepdims=True
    )
    cols = lax.broadcasted_iota(jnp.int32, (tok, 2 * tok), 1).astype(jnp.float32)
    return turned <= cols - tok


def convolve(last, last_row, skip, ahead, behind, gate, gate_prev, glin, glin_next,
             feats, upstream, source, tail, taps):
    tok, channels = upstream.shape
    steps = channels // LANES
    groups = LANES // GROUP

    def part(rows, p):
        return pl.BlockSpec((rows, LANES), lambda i: (0, i + p * steps))

    def fixed(shape):
        return pl.BlockSpec(shape, lambda i: (0, 0))

    own = part(tok, 0)
    f32 = jnp.float32
    return pl.pallas_call(
        functools.partial(conv_kernel, steps),
        grid=(steps,),
        in_specs=[fixed((tok, 1)), fixed((1, 2 * tok)), part(1, 0)]
        + [pl.BlockSpec((groups, 2 * tok), lambda i: (i, 0))] * 2
        + [own] * 8
        + [part(tok, p) for p in range(3)]
        + [part(16, p) for p in range(3)]
        + [part(SHORT, p) for p in range(3)],
        out_specs=[
            own,
            fixed((tok, 3 * channels)),
            fixed((8, 3 * channels)),
            fixed((8, 3 * channels)),
            fixed((SHORT, 3 * channels)),
            part(1, 0),
            pl.BlockSpec((groups, LEN), lambda i: (i, 0)),
        ],
        out_shape=[
            jax.ShapeDtypeStruct((tok, channels), jnp.bfloat16),
            jax.ShapeDtypeStruct((tok, 3 * channels), jnp.bfloat16),
            jax.ShapeDtypeStruct((8, 3 * channels), f32),
            jax.ShapeDtypeStruct((8, 3 * channels), f32),
            jax.ShapeDtypeStruct((SHORT, 3 * channels), f32),
            jax.ShapeDtypeStruct((1, channels), f32),
            jax.ShapeDtypeStruct((channels // GROUP, LEN), f32),
        ],
        compiler_params=pltpu.CompilerParams(vmem_limit_bytes=48 << 20),
        name="convolve",
    )(last, last_row, skip, ahead, behind, gate, gate_prev, glin, glin_next, *feats, upstream,
      source, source, source, tail, tail, tail, taps, taps, taps)


def reduce_kernel(
    m, n, scaling, x, out, pair, mine, parts, result, send0, recv0, send1, recv1, send2, recv2
):
    me, half = lax.axis_index("ctx"), lax.axis_index("fsdp")
    barrier = pltpu.get_barrier_semaphore()

    def greet_share(i, carry):
        pl.semaphore_signal(
            barrier, inc=1, device_id=(me, lax.rem(half + i, m)), device_id_type=MESH
        )
        return carry

    def greet(i, carry):
        pl.semaphore_signal(
            barrier, inc=1, device_id=(lax.rem(me + i, n), half), device_id_type=MESH
        )
        return carry

    lax.fori_loop(1, m, greet_share, 0)
    lax.fori_loop(1, n, greet, 0)
    pl.semaphore_wait(barrier, m + n - 2)

    def started(make, stop):
        def run(i, carry):
            make(i).start()
            return carry
        lax.fori_loop(1, stop, run, 0)

    def waited(make, stop):
        def run(i, carry):
            make(i).wait()
            return carry
        lax.fori_loop(1, stop, run, 0)

    def share(i):
        to = lax.rem(half + i, m)
        return pltpu.make_async_remote_copy(
            src_ref=x.at[to], dst_ref=pair.at[i], send_sem=send0.at[i], recv_sem=recv0.at[i],
            device_id=(me, to), device_id_type=MESH,
        )

    started(share, m)
    waited(share, m)
    owned = lax.fori_loop(1, m, lambda i, total: total + pair[i], x[half])
    mine[...] = (owned * scaling).astype(jnp.bfloat16)

    def scatter(i):
        to = lax.rem(me + i, n)
        return pltpu.make_async_remote_copy(
            src_ref=mine.at[to], dst_ref=parts.at[i], send_sem=send1.at[i], recv_sem=recv1.at[i],
            device_id=(to, half), device_id_type=MESH,
        )

    def gather(i):
        return pltpu.make_async_remote_copy(
            src_ref=result.at[me], dst_ref=result.at[me], send_sem=send2.at[i],
            recv_sem=recv2.at[i], device_id=(lax.rem(me + i, n), half), device_id_type=MESH,
        )

    started(scatter, n)
    waited(scatter, n)

    def add(i, total):
        return total + parts[i].astype(jnp.float32)

    total = lax.fori_loop(1, n, add, mine[me].astype(jnp.float32))
    result[me] = total.astype(jnp.bfloat16)
    started(gather, n)
    waited(gather, n)
    out[...] = result[...].astype(jnp.float32)


def reduced(packed, scaling):
    m, n, rows, _ = packed.shape
    half = pltpu.VMEM((n, rows, LANES), jnp.bfloat16)
    return pl.pallas_call(
        functools.partial(reduce_kernel, m, n, scaling),
        in_specs=[pl.BlockSpec(memory_space=pltpu.VMEM)],
        out_specs=pl.BlockSpec(memory_space=pltpu.VMEM),
        out_shape=jax.ShapeDtypeStruct((n, rows, LANES), jnp.float32),
        scratch_shapes=[
            pltpu.VMEM((m, n, rows, LANES), jnp.float32),
            half,
            half,
            half,
            pltpu.SemaphoreType.DMA((m,)),
            pltpu.SemaphoreType.DMA((m,)),
            pltpu.SemaphoreType.DMA((n,)),
            pltpu.SemaphoreType.DMA((n,)),
            pltpu.SemaphoreType.DMA((n,)),
            pltpu.SemaphoreType.DMA((n,)),
        ],
        compiler_params=pltpu.CompilerParams(
            collective_id=0, has_side_effects=True, vmem_limit_bytes=32 << 20
        ),
        name="reduce",
    )(packed)


def body(proj, short_taps, long_filter, skip, grad_out, starts):
    source, upstream = proj[0], grad_out[0]
    tok, channels = upstream.shape
    count, me = lax.axis_size("ctx"), lax.axis_index("ctx")
    pairs = lax.axis_size("fsdp")
    taps = lax.all_gather(short_taps, "fsdp", axis=1, tiled=True)
    filt = lax.all_gather(long_filter, "fsdp", axis=1, tiled=True)
    factor = lax.all_gather(skip, "fsdp", axis=0, tiled=True)
    lists = lax.all_gather(starts[0, 0], "ctx")
    tail = passed_along(source[tok - 16 :], "ctx", 1)
    places = jnp.arange(count, dtype=jnp.int32)
    positions = jnp.arange(tok, dtype=jnp.int32)
    absolute = jnp.where(lists < tok, lists + (places * tok)[:, None], -FAR)

    def last_of(device):
        first = device * tok
        seen = jnp.where(
            (absolute.reshape(-1)[None, :] <= first + positions[:, None]),
            absolute.reshape(-1)[None, :], -FAR,
        )
        return jnp.max(seen, axis=1) - first

    last = last_of(me)
    later = jnp.where(me < count - 1, last_of(me + 1) + tok, FAR)
    last_row = jnp.concatenate([last, later])[None, :]
    last = last[:, None]
    rows = filt.T
    empty = jnp.zeros_like(rows)
    ahead = jnp.concatenate([rows[:, ::-1], empty], axis=1)
    behind = jnp.concatenate([rows, empty], axis=1)

    qf, kf, vf, gate, glin = featurize(last, source, tail, taps, upstream)
    gate_prev = passed_along(gate, "ctx", 1)
    glin_next = passed_along(glin, "ctx", -1)
    mixed, grads, low, edge, short, skip_part, lag = convolve(
        last, last_row, factor[None], ahead, behind, gate, gate_prev, glin, glin_next,
        (qf, kf, vf), upstream, source, tail, taps,
    )
    returned = passed_along(edge[8 - (SHORT - 1) :].astype(jnp.bfloat16), "ctx", -1)
    fixed = low[8 - (SHORT - 1) :] + returned.astype(jnp.float32)
    grads = lax.dynamic_update_slice(grads, fixed.astype(jnp.bfloat16), (tok - (SHORT - 1), 0))

    scaling = float(pairs * count * tok) ** (-0.5)
    own = 3 * channels // pairs
    groups = channels // GROUP
    long_grad = lag[:, ::-1].T
    sizes = (SHORT * own, LEN * (groups // pairs), channels // pairs)
    flat = jnp.concatenate(
        [
            short.reshape(SHORT, pairs, own).transpose(1, 0, 2).reshape(pairs, -1),
            long_grad.reshape(LEN, pairs, groups // pairs).transpose(1, 0, 2).reshape(pairs, -1),
            skip_part.reshape(pairs, -1),
        ],
        axis=1,
    )
    unit = count * 16 * LANES
    padded = -(-flat.shape[1] // unit) * unit
    flat = jnp.pad(flat, ((0, 0), (0, padded - flat.shape[1])))
    summed = reduced(flat.reshape(pairs, count, -1, LANES), scaling).reshape(-1)
    a, b, c = sizes
    return (
        mixed[None],
        grads[None],
        summed[:a].reshape(SHORT, own),
        summed[a : a + b].reshape(LEN, groups // pairs),
        summed[a + b : a + b + c],
    )


def solution(mesh):
    window = P("fsdp", "ctx", None)
    return jax.shard_map(
        body,
        mesh=mesh,
        in_specs=(window, P(None, "fsdp"), P(None, "fsdp"), P("fsdp"), window, window),
        out_specs=(window, window, P(None, "fsdp"), P(None, "fsdp"), P("fsdp")),
        check_vma=False,
    )
```

```python
import functools

import jax
import jax.numpy as jnp
from jax import lax
from jax.experimental import pallas as pl
from jax.experimental.pallas import tpu as pltpu
from jax.sharding import PartitionSpec as P

GROUP = 16
LEN = 128
SHORT = 7
LANES = 128
FAR = 1 << 29
CHUNKS = 4
MESH = pl.DeviceIdType.MESH


def passed_along(block, axis, distance):
    devices = range(lax.axis_size(axis))
    route = [(i - distance, i) for i in devices if i - distance in devices]
    return lax.ppermute(block, axis, route)


def links(last):
    rows = lax.broadcasted_iota(jnp.int32, (last.shape[0], 1), 0)
    return [last <= rows - offset for offset in range(SHORT)]


def shifted_rows(tail, cur):
    whole = jnp.concatenate([tail[8:16].astype(jnp.float32), cur.astype(jnp.float32)], axis=0)
    return [
        (pltpu.roll(whole, offset, 0) if offset else whole)[8:] for offset in range(SHORT)
    ]


def exchange_matrix(size):
    r = lax.broadcasted_iota(jnp.int32, (size, size), 0)
    c = lax.broadcasted_iota(jnp.int32, (size, size), 1)
    return (r + c == size - 1).astype(jnp.bfloat16)


def featurize_kernel(last, q, k, v, qt, kt, vt, qw, kw, vw, up, qf, kf, vf, gate, glin):
    linked = links(last[...])

    def feature(cur, tail, taps):
        total = None
        for offset, rows in enumerate(shifted_rows(tail[...], cur[...])):
            term = taps[offset : offset + 1, :] * jnp.where(linked[offset], rows, 0.0)
            total = term if total is None else total + term
        return total

    query = feature(q, qt, qw)
    qf[...] = query
    key = feature(k, kt, kw)
    kf[...] = key
    value = feature(v, vt, vw)
    vf[...] = value
    gate[...] = (key * value).astype(jnp.bfloat16)
    through = (up[...].astype(jnp.float32) * query).astype(jnp.bfloat16)
    turned = jnp.dot(exchange_matrix(through.shape[0]), through, preferred_element_type=jnp.float32)
    glin[...] = turned.astype(jnp.bfloat16)


def featurize(chunk, chunks, last, source, tail, taps, upstream):
    tok, channels = upstream.shape
    width = min(512, channels // chunks)
    whole = channels // width
    steps = whole // chunks
    channels = channels // chunks

    def part(rows, p):
        return pl.BlockSpec((rows, width), lambda i: (0, i + chunk * steps + p * whole))

    own = pl.BlockSpec((tok, width), lambda i: (0, i))
    f32 = jax.ShapeDtypeStruct((tok, channels), jnp.float32)
    half = jax.ShapeDtypeStruct((tok, channels), jnp.bfloat16)
    return pl.pallas_call(
        featurize_kernel,
        grid=(steps,),
        in_specs=[pl.BlockSpec((tok, 1), lambda i: (0, 0))]
        + [part(tok, p) for p in range(3)]
        + [part(16, p) for p in range(3)]
        + [part(SHORT, p) for p in range(3)]
        + [part(tok, 0)],
        out_specs=[own] * 5,
        out_shape=[f32, f32, f32, half, half],
        compiler_params=pltpu.CompilerParams(vmem_limit_bytes=40 << 20),
        name="featurize",
    )(last, source, source, source, tail, tail, tail, taps, taps, taps, upstream)


def conv_kernel(
    last, last_turned, row_turned, skip, ahead, gate, gate_prev, glin, glin_next,
    qf, kf, vf, up, q, k, v, qt, kt, vt, qw, kw, vw,
    mixed, gq, gk, gv, low, edge, short, skip_out, lag, tiles_f, tiles_b, picked,
):
    tok = gate.shape[0]
    count = LANES // GROUP
    linked = links(last[...])
    cols = lax.broadcasted_iota(jnp.int32, (tok, tok), 1)
    rows = lax.broadcasted_iota(jnp.int32, (tok, tok), 0)
    below = cols <= rows
    fwd_prev = jnp.logical_and(jnp.logical_not(below), last[...] <= cols - tok)
    fwd_own = jnp.logical_and(below, last[...] <= cols)
    turned = tok - 1 - rows
    bwd_next = jnp.logical_and(jnp.logical_not(below), row_turned[:, :tok] <= turned)
    bwd_own = jnp.logical_and(below, row_turned[:, tok:] <= turned)
    lag_prev = jnp.logical_and(cols > turned, last_turned[...] <= cols - tok)
    lag_own = jnp.logical_and(cols <= turned, last_turned[...] <= cols)
    own_gate, own_glin = gate[...], glin[...]
    gate_win = jnp.concatenate([gate_prev[...], own_gate], axis=0)
    glin_win = jnp.concatenate([glin_next[...], own_glin], axis=0)
    lane = lax.broadcasted_iota(jnp.int32, (tok, LANES), 1) // GROUP
    for g in range(count):
        at = slice(g * tok, (g + 1) * tok)
        tile = jnp.broadcast_to(ahead[g : g + 1, :], (tok, LEN))
        tile = pltpu.roll(tile, 1, 1, stride=1, stride_axis=0)
        tiles_f[at, :tok] = jnp.where(fwd_prev, tile, 0.0).astype(jnp.bfloat16)
        tiles_f[at, tok:] = jnp.where(fwd_own, tile, 0.0).astype(jnp.bfloat16)
        tiles_b[at, :tok] = jnp.where(bwd_next, tile, 0.0).astype(jnp.bfloat16)
        tiles_b[at, tok:] = jnp.where(bwd_own, tile, 0.0).astype(jnp.bfloat16)
        picked[at, :] = jnp.where(lane == g, own_glin.astype(jnp.float32), 0.0).astype(jnp.bfloat16)
    out_f = jnp.dot(tiles_f[...], gate_win, preferred_element_type=jnp.float32)
    out_b = jnp.dot(tiles_b[...], glin_win, preferred_element_type=jnp.float32)
    product = lax.dot_general(
        picked[...], gate_win, (((1,), (1,)), ((), ())), preferred_element_type=jnp.float32
    )
    long_out, spread = out_f[:tok], out_b[:tok]
    for g in range(count):
        at = slice(g * tok, (g + 1) * tok)
        if g:
            long_out = jnp.where(lane == g, out_f[at], long_out)
            spread = jnp.where(lane == g, out_b[at], spread)
        folded = jnp.where(lag_prev, product[at, :tok], 0.0)
        folded = jnp.where(lag_own, product[at, tok:], folded)
        folded = pltpu.roll(folded, 0, 1, stride=1, stride_axis=0)
        lag[g : g + 1, :] = jnp.sum(folded, axis=0, keepdims=True)
    flip = exchange_matrix(tok)
    high = spread.astype(jnp.bfloat16)
    rest = (spread - high.astype(jnp.float32)).astype(jnp.bfloat16)
    spread = jnp.dot(flip, high, preferred_element_type=jnp.float32) + jnp.dot(
        flip, rest, preferred_element_type=jnp.float32
    )
    gate_f = own_gate.astype(jnp.float32)
    query, key, value = qf[...], kf[...], vf[...]
    upstream = up[...].astype(jnp.float32)
    factor = skip[...]
    combined = long_out + factor * gate_f
    mixed[...] = (query * combined).astype(jnp.bfloat16)
    through = upstream * query
    skip_out[...] = jnp.sum(through * gate_f, axis=0, keepdims=True)
    grad_gate = spread + factor * through
    feats = (upstream * combined, grad_gate * value, grad_gate * key)
    for part, (grad, cur, tail, taps, out) in enumerate(
        zip(feats, (q, k, v), (qt, kt, vt), (qw, kw, vw), (gq, gk, gv))
    ):
        total = None
        for offset, earlier in enumerate(shifted_rows(tail[...], cur[...])):
            kept = jnp.where(linked[offset], grad, 0.0)
            short[part, offset : offset + 1, :] = jnp.sum(kept * earlier, axis=0, keepdims=True)
            moved = jnp.concatenate(
                [jnp.zeros((8, LANES), jnp.float32), taps[offset : offset + 1, :] * kept], axis=0
            )
            if offset:
                moved = pltpu.roll(moved, tok + 8 - offset, 0)
            total = moved if total is None else total + moved
        out[...] = total[8:].astype(jnp.bfloat16)
        low[part] = total[tok:]
        edge[part] = total[:8]


def convolve(chunk, chunks, last, last_turned, row_turned, skip, ahead, gate, gate_prev, glin,
             glin_next, feats, upstream, source, tail, taps):
    tok, channels = upstream.shape
    whole = channels // LANES
    steps = whole // chunks
    channels = channels // chunks
    groups = LANES // GROUP

    def part(rows, p):
        return pl.BlockSpec((rows, LANES), lambda i: (0, i + chunk * steps + p * whole))

    def fixed(shape):
        return pl.BlockSpec(shape, lambda i: (0, 0))

    def three(rows):
        return pl.BlockSpec((3, rows, LANES), lambda i: (0, 0, i))

    own = pl.BlockSpec((tok, LANES), lambda i: (0, i))
    f32 = jnp.float32
    half = jax.ShapeDtypeStruct((tok, channels), jnp.bfloat16)
    rows = 2 * groups * tok * channels * 2 * tok
    return pl.pallas_call(
        conv_kernel,
        grid=(steps,),
        in_specs=[fixed((tok, 1)), fixed((tok, 1)), fixed((1, 2 * tok)), part(1, 0)]
        + [pl.BlockSpec((groups, LEN), lambda i: (i + chunk * steps, 0))]
        + [own] * 7
        + [part(tok, 0)]
        + [part(tok, p) for p in range(3)]
        + [part(16, p) for p in range(3)]
        + [part(SHORT, p) for p in range(3)],
        out_specs=[own] * 4
        + [three(8), three(8), three(SHORT)]
        + [pl.BlockSpec((1, LANES), lambda i: (0, i)), pl.BlockSpec((groups, LEN), lambda i: (i, 0))],
        out_shape=[half] * 4 + [
            jax.ShapeDtypeStruct((3, 8, channels), f32),
            jax.ShapeDtypeStruct((3, 8, channels), f32),
            jax.ShapeDtypeStruct((3, SHORT, channels), f32),
            jax.ShapeDtypeStruct((1, channels), f32),
            jax.ShapeDtypeStruct((channels // GROUP, LEN), f32),
        ],
        scratch_shapes=[
            pltpu.VMEM((groups * tok, 2 * tok), jnp.bfloat16),
            pltpu.VMEM((groups * tok, 2 * tok), jnp.bfloat16),
            pltpu.VMEM((groups * tok, LANES), jnp.bfloat16),
        ],
        compiler_params=pltpu.CompilerParams(vmem_limit_bytes=40 << 20),
        cost_estimate=pl.CostEstimate(flops=3 * rows, bytes_accessed=22 * tok * channels, transcendentals=0),
        name="convolve",
    )(last, last_turned, row_turned, skip, ahead, gate, gate_prev, glin, glin_next, *feats,
      upstream, source, source, source, tail, tail, tail, taps, taps, taps)


def entry_kernel(m, n, proj, taps, filt, skip, starts, tail, taps_all, filt_all, skip_all, lists,
                 tail_sems, start_send, start_recv, share_send, share_recv):
    me, half = lax.axis_index("ctx"), lax.axis_index("fsdp")
    tok, own, skips = proj.shape[0], taps.shape[1], skip.shape[1]
    barrier = pltpu.get_barrier_semaphore()

    def greet_share(i, carry):
        pl.semaphore_signal(
            barrier, inc=1, device_id=(me, lax.rem(half + i, m)), device_id_type=MESH
        )
        return carry

    def greet(i, carry):
        pl.semaphore_signal(
            barrier, inc=1, device_id=(lax.rem(me + i, n), half), device_id_type=MESH
        )
        return carry

    lax.fori_loop(1, m, greet_share, 0)
    lax.fori_loop(1, n, greet, 0)
    pl.semaphore_wait(barrier, m + n - 2)
    taps_at = pl.ds(pl.multiple_of(half * own, LANES), own)
    skip_at = pl.ds(pl.multiple_of(half * skips, LANES), skips)

    def first(i):
        return pltpu.make_async_remote_copy(
            src_ref=starts, dst_ref=lists.at[me], send_sem=start_send.at[i],
            recv_sem=start_recv.at[i], device_id=(lax.rem(me + i, n), half), device_id_type=MESH,
        )

    def shares(i):
        to = lax.rem(half + i, m)
        pairs = (
            (taps, taps_all.at[:, taps_at]),
            (filt, filt_all.at[half]),
            (skip, skip_all.at[:, skip_at]),
        )
        return [
            pltpu.make_async_remote_copy(
                src_ref=src, dst_ref=dst, send_sem=share_send.at[j, i],
                recv_sem=share_recv.at[j, i], device_id=(me, to), device_id_type=MESH,
            )
            for j, (src, dst) in enumerate(pairs)
        ]

    onward = pltpu.make_async_remote_copy(
        src_ref=proj.at[tok - 16 : tok], dst_ref=tail, send_sem=tail_sems.at[0],
        recv_sem=tail_sems.at[1], device_id=(lax.rem(me + 1, n), half), device_id_type=MESH,
    )
    onward.start()

    def start_first(i, carry):
        first(i).start()
        return carry

    def start_share(i, carry):
        for copy in shares(i):
            copy.start()
        return carry

    def wait_first(i, carry):
        first(i).wait()
        return carry

    def wait_share(i, carry):
        for copy in shares(i):
            copy.wait()
        return carry

    lax.fori_loop(1, n, start_first, 0)
    lax.fori_loop(1, m, start_share, 0)
    lists[me] = starts[...]
    taps_all[:, taps_at] = taps[...]
    filt_all[half] = filt[...]
    skip_all[:, skip_at] = skip[...]
    lax.fori_loop(1, n, wait_first, 0)
    lax.fori_loop(1, m, wait_share, 0)
    onward.wait()


def entry(m, n, source, taps, filt, skip, starts):
    vmem = pl.BlockSpec(memory_space=pltpu.VMEM)
    f32 = jnp.float32
    return pl.pallas_call(
        functools.partial(entry_kernel, m, n),
        in_specs=[pl.BlockSpec(memory_space=pl.ANY)] + [vmem] * 4,
        out_specs=[vmem] * 5,
        out_shape=[
            jax.ShapeDtypeStruct((16, source.shape[1]), source.dtype),
            jax.ShapeDtypeStruct((SHORT, m * taps.shape[1]), f32),
            jax.ShapeDtypeStruct((m,) + filt.shape, f32),
            jax.ShapeDtypeStruct((1, m * skip.shape[1]), f32),
            jax.ShapeDtypeStruct((n,) + starts.shape, jnp.int32),
        ],
        scratch_shapes=[
            pltpu.SemaphoreType.DMA((2,)),
            pltpu.SemaphoreType.DMA((n,)),
            pltpu.SemaphoreType.DMA((n,)),
            pltpu.SemaphoreType.DMA((3, m)),
            pltpu.SemaphoreType.DMA((3, m)),
        ],
        compiler_params=pltpu.CompilerParams(
            collective_id=1, has_side_effects=True, vmem_limit_bytes=16 << 20
        ),
        name="entry",
    )(source, taps, filt, skip, starts)


def reduce_kernel(
    m, n, scaling, x, out, pair, mine, parts, result, send0, recv0, send1, recv1, send2, recv2
):
    me, half = lax.axis_index("ctx"), lax.axis_index("fsdp")
    barrier = pltpu.get_barrier_semaphore()

    def greet_share(i, carry):
        pl.semaphore_signal(
            barrier, inc=1, device_id=(me, lax.rem(half + i, m)), device_id_type=MESH
        )
        return carry

    def greet(i, carry):
        pl.semaphore_signal(
            barrier, inc=1, device_id=(lax.rem(me + i, n), half), device_id_type=MESH
        )
        return carry

    lax.fori_loop(1, m, greet_share, 0)
    lax.fori_loop(1, n, greet, 0)
    pl.semaphore_wait(barrier, m + n - 2)

    def started(make, stop):
        def run(i, carry):
            make(i).start()
            return carry
        lax.fori_loop(1, stop, run, 0)

    def waited(make, stop):
        def run(i, carry):
            make(i).wait()
            return carry
        lax.fori_loop(1, stop, run, 0)

    def share(i):
        to = lax.rem(half + i, m)
        return pltpu.make_async_remote_copy(
            src_ref=x.at[to], dst_ref=pair.at[i], send_sem=send0.at[i], recv_sem=recv0.at[i],
            device_id=(me, to), device_id_type=MESH,
        )

    started(share, m)
    waited(share, m)
    owned = lax.fori_loop(1, m, lambda i, total: total + pair[i], x[half])
    mine[...] = (owned * scaling).astype(jnp.bfloat16)

    def scatter(i):
        to = lax.rem(me + i, n)
        return pltpu.make_async_remote_copy(
            src_ref=mine.at[to], dst_ref=parts.at[i], send_sem=send1.at[i], recv_sem=recv1.at[i],
            device_id=(to, half), device_id_type=MESH,
        )

    def gather(i):
        return pltpu.make_async_remote_copy(
            src_ref=result.at[me], dst_ref=result.at[me], send_sem=send2.at[i],
            recv_sem=recv2.at[i], device_id=(lax.rem(me + i, n), half), device_id_type=MESH,
        )

    started(scatter, n)
    waited(scatter, n)

    def add(i, total):
        return total + parts[i].astype(jnp.float32)

    total = lax.fori_loop(1, n, add, mine[me].astype(jnp.float32))
    result[me] = total.astype(jnp.bfloat16)
    started(gather, n)
    waited(gather, n)
    out[...] = result[...].astype(jnp.float32)


def reduced(packed, scaling):
    m, n, rows, _ = packed.shape
    half = pltpu.VMEM((n, rows, LANES), jnp.bfloat16)
    return pl.pallas_call(
        functools.partial(reduce_kernel, m, n, scaling),
        in_specs=[pl.BlockSpec(memory_space=pltpu.VMEM)],
        out_specs=pl.BlockSpec(memory_space=pltpu.VMEM),
        out_shape=jax.ShapeDtypeStruct((n, rows, LANES), jnp.float32),
        scratch_shapes=[
            pltpu.VMEM((m, n, rows, LANES), jnp.float32),
            half,
            half,
            half,
            pltpu.SemaphoreType.DMA((m,)),
            pltpu.SemaphoreType.DMA((m,)),
            pltpu.SemaphoreType.DMA((n,)),
            pltpu.SemaphoreType.DMA((n,)),
            pltpu.SemaphoreType.DMA((n,)),
            pltpu.SemaphoreType.DMA((n,)),
        ],
        compiler_params=pltpu.CompilerParams(
            collective_id=0, has_side_effects=True, vmem_limit_bytes=32 << 20
        ),
        name="reduce",
    )(packed)


def body(proj, short_taps, long_filter, skip, grad_out, starts):
    source, upstream = proj[0], grad_out[0]
    tok, channels = upstream.shape
    count, me = lax.axis_size("ctx"), lax.axis_index("ctx")
    pairs = lax.axis_size("fsdp")
    listed = jnp.pad(starts[0], ((0, 7), (0, LANES - starts.shape[2])), constant_values=tok)
    tail, taps, filt, factor, lists = entry(
        pairs, count, source, short_taps, long_filter, skip[None], listed
    )
    lists = lists[:, 0, : starts.shape[2]]
    places = jnp.arange(count, dtype=jnp.int32)
    positions = jnp.arange(tok, dtype=jnp.int32)
    absolute = jnp.where(lists < tok, lists + (places * tok)[:, None], -FAR)

    def last_of(device):
        first = device * tok
        seen = jnp.where(
            (absolute.reshape(-1)[None, :] <= first + positions[:, None]),
            absolute.reshape(-1)[None, :], -FAR,
        )
        return jnp.max(seen, axis=1) - first

    last = last_of(me)
    later = jnp.where(me < count - 1, last_of(me + 1) + tok, FAR)
    row_turned = jnp.concatenate([later[::-1], last[::-1]])[None, :]
    last_turned = last[::-1][:, None]
    last = last[:, None]
    ahead = filt[:, ::-1].transpose(0, 2, 1).reshape(-1, LEN)

    chunks = min(CHUNKS, channels // LANES)
    made = [featurize(c, chunks, last, source, tail, taps, upstream) for c in range(chunks)]
    moved = [
        (passed_along(gate, "ctx", 1), passed_along(glin, "ctx", -1))
        for _, _, _, gate, glin in made
    ]
    parts = [
        convolve(
            c, chunks, last, last_turned, row_turned, factor, ahead, gate, gate_prev, glin,
            glin_next, (qf, kf, vf), upstream, source, tail, taps,
        )
        for c, ((qf, kf, vf, gate, glin), (gate_prev, glin_next)) in enumerate(zip(made, moved))
    ]
    mixed = jnp.concatenate([part[0] for part in parts], axis=1)
    low, edge, short = (
        jnp.concatenate([part[i] for part in parts], axis=2).transpose(1, 0, 2).reshape(
            -1, 3 * channels
        )
        for i in (4, 5, 6)
    )
    skip_part = jnp.concatenate([part[7] for part in parts], axis=1)
    lag = jnp.concatenate([part[8] for part in parts], axis=0)
    grads = jnp.concatenate([part[i] for i in (1, 2, 3) for part in parts], axis=1)
    returned = passed_along(edge[8 - (SHORT - 1) :].astype(jnp.bfloat16), "ctx", -1)
    fixed = low[8 - (SHORT - 1) :] + returned.astype(jnp.float32)
    grads = lax.dynamic_update_slice(grads, fixed.astype(jnp.bfloat16), (tok - (SHORT - 1), 0))

    scaling = float(pairs * count * tok) ** (-0.5)
    own = 3 * channels // pairs
    groups = channels // GROUP
    long_grad = lag[:, ::-1].T
    sizes = (SHORT * own, LEN * (groups // pairs), channels // pairs)
    flat = jnp.concatenate(
        [
            short.reshape(SHORT, pairs, own).transpose(1, 0, 2).reshape(pairs, -1),
            long_grad.reshape(LEN, pairs, groups // pairs).transpose(1, 0, 2).reshape(pairs, -1),
            skip_part.reshape(pairs, -1),
        ],
        axis=1,
    )
    unit = count * 16 * LANES
    padded = -(-flat.shape[1] // unit) * unit
    flat = jnp.pad(flat, ((0, 0), (0, padded - flat.shape[1])))
    summed = reduced(flat.reshape(pairs, count, -1, LANES), scaling).reshape(-1)
    a, b, c = sizes
    return (
        mixed[None],
        grads[None],
        summed[:a].reshape(SHORT, own),
        summed[a : a + b].reshape(LEN, groups // pairs),
        summed[a + b : a + b + c],
    )


def solution(mesh):
    window = P("fsdp", "ctx", None)
    return jax.shard_map(
        body,
        mesh=mesh,
        in_specs=(window, P(None, "fsdp"), P(None, "fsdp"), P("fsdp"), window, window),
        out_specs=(window, window, P(None, "fsdp"), P(None, "fsdp"), P("fsdp")),
        check_vma=False,
    )
```

```python
import functools

import jax
import jax.numpy as jnp
from jax import lax
from jax.experimental import pallas as pl
from jax.experimental.pallas import tpu as pltpu
from jax.sharding import PartitionSpec as P

GROUP = 16
LEN = 128
SHORT = 7
LANES = 128
FAR = 1 << 29
MESH = pl.DeviceIdType.MESH


def passed_along(block, axis, distance):
    devices = range(lax.axis_size(axis))
    route = [(i - distance, i) for i in devices if i - distance in devices]
    return lax.ppermute(block, axis, route)


def exchange_matrix(size):
    r = lax.broadcasted_iota(jnp.int32, (size, size), 0)
    c = lax.broadcasted_iota(jnp.int32, (size, size), 1)
    return (r + c == size - 1).astype(jnp.bfloat16)


def operator_kernel(
    n, per, last, last_turned, row_turned, skip, ahead, proj, tail, taps, up,
    mixed, grads, low, edge, short, skip_out, lag,
    feats, gate, glin, gate_prev, glin_next, pad, spill, tiles_f, tiles_b, picked,
    gate_send, gate_recv, glin_send, glin_recv,
):
    me, half = lax.axis_index("ctx"), lax.axis_index("fsdp")
    right, left = lax.rem(me + 1, n), lax.rem(me + n - 1, n)
    blocks, tok = gate.shape[0], gate.shape[1]
    chunks, count = blocks // per, LANES // GROUP
    f32, bf16 = jnp.float32, jnp.bfloat16
    barrier = pltpu.get_barrier_semaphore()
    for to in (left, right):
        pl.semaphore_signal(barrier, inc=1, device_id=(to, half), device_id_type=MESH)
    pl.semaphore_wait(barrier, 2)
    rows = lax.broadcasted_iota(jnp.int32, (tok, LANES), 0)
    cols = lax.broadcasted_iota(jnp.int32, (tok, LANES), 1)
    spill[:, 0:8, :] = jnp.zeros((SHORT, 8, LANES), f32)
    spill[:, tok + 8 :, :] = jnp.zeros((SHORT, 8, LANES), f32)

    def lanes(block, part=0):
        return pl.ds(pl.multiple_of((part * blocks + block) * LANES, LANES), LANES)

    def copies(chunk):
        at = pl.ds(chunk * per, per)
        return (
            pltpu.make_async_remote_copy(
                src_ref=gate.at[at], dst_ref=gate_prev.at[at], send_sem=gate_send.at[chunk],
                recv_sem=gate_recv.at[chunk], device_id=(right, half), device_id_type=MESH,
            ),
            pltpu.make_async_remote_copy(
                src_ref=glin.at[at], dst_ref=glin_next.at[at], send_sem=glin_send.at[chunk],
                recv_sem=glin_recv.at[chunk], device_id=(left, half), device_id_type=MESH,
            ),
        )

    def load_rows(block):
        for part in range(3):
            at = lanes(block, part)
            pad[part, 0:8, :] = tail[:, at].astype(f32)[8:16]
            pad[part, 8:, :] = proj[:, at].astype(f32)

    def earlier(part, offset):
        return pad[part, 8 - offset : 8 - offset + tok, :]

    def featurize(block, carry):
        load_rows(block)
        made = []
        for part in range(3):
            at = lanes(block, part)
            total = jnp.zeros((tok, LANES), f32)
            for offset in range(SHORT):
                kept = jnp.where(last[...] <= rows - offset, earlier(part, offset), 0.0)
                total = total + taps[offset : offset + 1, at] * kept
            feats[part, block] = total
            made.append(total)
        gate[block] = (made[1] * made[2]).astype(bf16)
        through = (up[:, lanes(block)].astype(f32) * made[0]).astype(bf16)
        turned = jnp.dot(exchange_matrix(tok), through, preferred_element_type=f32)
        glin[block] = turned.astype(bf16)
        return carry

    def prepare(chunk, carry):
        lax.fori_loop(chunk * per, (chunk + 1) * per, featurize, 0)
        for copy in copies(chunk):
            copy.start()
        return carry

    lax.fori_loop(0, chunks, prepare, 0)

    def convolve(block, carry):
        at = lanes(block)
        start = last[...]
        start_turned = last_turned[...]
        below = cols <= rows
        fwd_prev = jnp.logical_and(cols > rows, start <= cols - tok)
        fwd_own = jnp.logical_and(below, start <= cols)
        turned = tok - 1 - rows
        bwd_next = jnp.logical_and(cols > rows, row_turned[0:1, :tok] <= turned)
        bwd_own = jnp.logical_and(below, row_turned[0:1, tok:] <= turned)
        lag_prev = jnp.logical_and(cols > turned, start_turned <= cols - tok)
        lag_own = jnp.logical_and(cols <= turned, start_turned <= cols)
        lane = cols // GROUP
        own_gate, own_glin = gate[block], glin[block]
        gate_win = jnp.concatenate([gate_prev[block], own_gate], axis=0)
        glin_win = jnp.concatenate([glin_next[block], own_glin], axis=0)
        glin_f = own_glin.astype(f32)
        filters = ahead[pl.ds(pl.multiple_of(block * count, count), count), :]
        for g in range(count):
            part = slice(g * tok, (g + 1) * tok)
            tile = jnp.broadcast_to(filters[g : g + 1, :], (tok, LEN))
            tile = pltpu.roll(tile, 1, 1, stride=1, stride_axis=0)
            tiles_f[part, :tok] = jnp.where(fwd_prev, tile, 0.0).astype(bf16)
            tiles_f[part, tok:] = jnp.where(fwd_own, tile, 0.0).astype(bf16)
            tiles_b[part, :tok] = jnp.where(bwd_next, tile, 0.0).astype(bf16)
            tiles_b[part, tok:] = jnp.where(bwd_own, tile, 0.0).astype(bf16)
            picked[part, :] = jnp.where(lane == g, glin_f, 0.0).astype(bf16)
        out_f = jnp.dot(tiles_f[...], gate_win, preferred_element_type=f32)
        out_b = jnp.dot(tiles_b[...], glin_win, preferred_element_type=f32)
        product = lax.dot_general(
            picked[...], gate_win, (((1,), (1,)), ((), ())), preferred_element_type=f32
        )
        long_out, spread = out_f[:tok], out_b[:tok]
        for g in range(count):
            part = slice(g * tok, (g + 1) * tok)
            if g:
                long_out = jnp.where(lane == g, out_f[part], long_out)
                spread = jnp.where(lane == g, out_b[part], spread)
            folded = jnp.where(lag_prev, product[part, :tok], 0.0)
            folded = jnp.where(lag_own, product[part, tok:], folded)
            folded = pltpu.roll(folded, 0, 1, stride=1, stride_axis=0)
            lag[block, g : g + 1, :] = jnp.sum(folded, axis=0, keepdims=True)
        flip = exchange_matrix(tok)
        high = spread.astype(bf16)
        rest = (spread - high.astype(f32)).astype(bf16)
        spread = jnp.dot(flip, high, preferred_element_type=f32) + jnp.dot(
            flip, rest, preferred_element_type=f32
        )
        gate_f = own_gate.astype(f32)
        query, key, value = feats[0, block], feats[1, block], feats[2, block]
        upstream = up[:, at].astype(f32)
        factor = skip[:, at]
        combined = long_out + factor * gate_f
        mixed[:, at] = (query * combined).astype(bf16)
        through = upstream * query
        skip_out[:, at] = jnp.sum(through * gate_f, axis=0, keepdims=True)
        grad_gate = spread + factor * through
        load_rows(block)
        for part, grad in enumerate((upstream * combined, grad_gate * value, grad_gate * key)):
            at = lanes(block, part)
            for offset in range(SHORT):
                kept = jnp.where(start <= rows - offset, grad, 0.0)
                short[offset : offset + 1, at] = jnp.sum(
                    kept * earlier(part, offset), axis=0, keepdims=True
                )
                spill[offset, 8 : tok + 8, :] = taps[offset : offset + 1, at] * kept
            total = spill[0, 0 : tok + 8, :]
            for offset in range(1, SHORT):
                total = total + spill[offset, offset : offset + tok + 8, :]
            grads[:, at] = total[8:].astype(bf16)
            low[:, at] = total[tok:]
            edge[:, at] = total[:8]
        return carry

    def use(chunk, carry):
        for copy in copies(chunk):
            copy.wait_recv()
        lax.fori_loop(chunk * per, (chunk + 1) * per, convolve, 0)
        return carry

    lax.fori_loop(0, chunks, use, 0)

    def sent(chunk, carry):
        for copy in copies(chunk):
            copy.wait_send()
        return carry

    lax.fori_loop(0, chunks, sent, 0)


def operate(n, last, last_turned, row_turned, skip, ahead, source, tail, taps, upstream):
    tok, channels = upstream.shape
    blocks = channels // LANES
    per = min(4, blocks)
    count = LANES // GROUP
    f32 = jnp.float32
    vmem = pl.BlockSpec(memory_space=pltpu.VMEM)
    half = pltpu.VMEM((blocks, tok, LANES), jnp.bfloat16)
    tiles = pltpu.VMEM((count * tok, 2 * tok), jnp.bfloat16)
    sems = pltpu.SemaphoreType.DMA((blocks // per,))
    return pl.pallas_call(
        functools.partial(operator_kernel, n, per),
        in_specs=[vmem] * 9,
        out_specs=[vmem] * 7,
        out_shape=[
            jax.ShapeDtypeStruct((tok, channels), jnp.bfloat16),
            jax.ShapeDtypeStruct((tok, 3 * channels), jnp.bfloat16),
            jax.ShapeDtypeStruct((8, 3 * channels), f32),
            jax.ShapeDtypeStruct((8, 3 * channels), f32),
            jax.ShapeDtypeStruct((SHORT, 3 * channels), f32),
            jax.ShapeDtypeStruct((1, channels), f32),
            jax.ShapeDtypeStruct((blocks, count, LEN), f32),
        ],
        scratch_shapes=[
            pltpu.VMEM((3, blocks, tok, LANES), f32),
            half,
            half,
            half,
            half,
            pltpu.VMEM((3, tok + 8, LANES), f32),
            pltpu.VMEM((SHORT, tok + 16, LANES), f32),
            tiles,
            tiles,
            pltpu.VMEM((count * tok, LANES), jnp.bfloat16),
            sems,
            sems,
            sems,
            sems,
        ],
        compiler_params=pltpu.CompilerParams(
            collective_id=2, has_side_effects=True, vmem_limit_bytes=48 << 20
        ),
        name="operate",
    )(last, last_turned, row_turned, skip, ahead, source, tail, taps, upstream)


def entry_kernel(m, n, proj, taps, filt, skip, starts, tail, taps_all, filt_all, skip_all,
                 last, last_turned, row_turned, lists, tail_sems, start_send, start_recv, share_send, share_recv):
    me, half = lax.axis_index("ctx"), lax.axis_index("fsdp")
    tok, width, skips = proj.shape[0], taps.shape[1], skip.shape[1]
    barrier = pltpu.get_barrier_semaphore()

    def greet_share(i, carry):
        pl.semaphore_signal(
            barrier, inc=1, device_id=(me, lax.rem(half + i, m)), device_id_type=MESH
        )
        return carry

    def greet(i, carry):
        pl.semaphore_signal(
            barrier, inc=1, device_id=(lax.rem(me + i, n), half), device_id_type=MESH
        )
        return carry

    lax.fori_loop(1, m, greet_share, 0)
    lax.fori_loop(1, n, greet, 0)
    pl.semaphore_wait(barrier, m + n - 2)
    taps_at = pl.ds(pl.multiple_of(half * width, LANES), width)
    skip_at = pl.ds(pl.multiple_of(half * skips, LANES), skips)

    def first(i):
        return pltpu.make_async_remote_copy(
            src_ref=starts, dst_ref=lists.at[me], send_sem=start_send.at[i],
            recv_sem=start_recv.at[i], device_id=(lax.rem(me + i, n), half), device_id_type=MESH,
        )

    def shares(i):
        to = lax.rem(half + i, m)
        pairs = (
            (taps, taps_all.at[:, taps_at]),
            (filt, filt_all.at[half]),
            (skip, skip_all.at[:, skip_at]),
        )
        return [
            pltpu.make_async_remote_copy(
                src_ref=src, dst_ref=dst, send_sem=share_send.at[j, i],
                recv_sem=share_recv.at[j, i], device_id=(me, to), device_id_type=MESH,
            )
            for j, (src, dst) in enumerate(pairs)
        ]

    onward = pltpu.make_async_remote_copy(
        src_ref=proj.at[tok - 16 : tok], dst_ref=tail, send_sem=tail_sems.at[0],
        recv_sem=tail_sems.at[1], device_id=(lax.rem(me + 1, n), half), device_id_type=MESH,
    )
    onward.start()

    def start_first(i, carry):
        first(i).start()
        return carry

    def start_share(i, carry):
        for copy in shares(i):
            copy.start()
        return carry

    def wait_first(i, carry):
        first(i).wait()
        return carry

    def wait_share(i, carry):
        for copy in shares(i):
            copy.wait()
        return carry

    lax.fori_loop(1, n, start_first, 0)
    lax.fori_loop(1, m, start_share, 0)
    lists[me] = starts[...]
    taps_all[:, taps_at] = taps[...]
    filt_all[half] = filt[...]
    skip_all[:, skip_at] = skip[...]
    lax.fori_loop(1, n, wait_first, 0)
    rows = lax.broadcasted_iota(jnp.int32, (tok, LANES), 0)
    cols = lax.broadcasted_iota(jnp.int32, (tok, LANES), 1)

    def latest(places):
        def look(j, best):
            listed = lists[j, 0:1, :]
            placed = jnp.where(listed < tok, listed + (j - me) * tok, -FAR)
            return jnp.maximum(best, jnp.where(placed <= places, placed, -FAR))

        best = lax.fori_loop(0, n, look, jnp.full((tok, LANES), -FAR, jnp.int32))
        top = jnp.max(best.astype(jnp.float32), axis=1, keepdims=True)
        return jnp.broadcast_to(top, (tok, LANES))

    def as_row(column):
        return jnp.sum(jnp.where(rows == cols, column, 0.0), axis=0, keepdims=True)

    own = latest(rows)
    turned = latest(tok - 1 - rows)
    later = latest(2 * tok - 1 - rows)
    last[...] = own.astype(jnp.int32)
    last_turned[...] = turned.astype(jnp.int32)
    later = jnp.where(me < n - 1, as_row(later).astype(jnp.int32), FAR)
    row_turned[:, :tok] = jnp.broadcast_to(later, (8, tok))
    row_turned[:, tok:] = jnp.broadcast_to(as_row(turned).astype(jnp.int32), (8, tok))
    lax.fori_loop(1, m, wait_share, 0)
    onward.wait()


def entry(m, n, source, taps, filt, skip, starts):
    vmem = pl.BlockSpec(memory_space=pltpu.VMEM)
    f32 = jnp.float32
    return pl.pallas_call(
        functools.partial(entry_kernel, m, n),
        in_specs=[pl.BlockSpec(memory_space=pl.ANY)] + [vmem] * 4,
        out_specs=[vmem] * 7,
        out_shape=[
            jax.ShapeDtypeStruct((16, source.shape[1]), source.dtype),
            jax.ShapeDtypeStruct((SHORT, m * taps.shape[1]), f32),
            jax.ShapeDtypeStruct((m,) + filt.shape, f32),
            jax.ShapeDtypeStruct((1, m * skip.shape[1]), f32),
            jax.ShapeDtypeStruct((source.shape[0], LANES), jnp.int32),
            jax.ShapeDtypeStruct((source.shape[0], LANES), jnp.int32),
            jax.ShapeDtypeStruct((8, 2 * source.shape[0]), jnp.int32),
        ],
        scratch_shapes=[
            pltpu.VMEM((n,) + starts.shape, jnp.int32),
            pltpu.SemaphoreType.DMA((2,)),
            pltpu.SemaphoreType.DMA((n,)),
            pltpu.SemaphoreType.DMA((n,)),
            pltpu.SemaphoreType.DMA((3, m)),
            pltpu.SemaphoreType.DMA((3, m)),
        ],
        compiler_params=pltpu.CompilerParams(
            collective_id=1, has_side_effects=True, vmem_limit_bytes=16 << 20
        ),
        name="entry",
    )(source, taps, filt, skip, starts)


def reduce_kernel(
    m, n, scaling, x, out, pair, mine, parts, result, send0, recv0, send1, recv1, send2, recv2
):
    me, half = lax.axis_index("ctx"), lax.axis_index("fsdp")
    barrier = pltpu.get_barrier_semaphore()

    def greet_share(i, carry):
        pl.semaphore_signal(
            barrier, inc=1, device_id=(me, lax.rem(half + i, m)), device_id_type=MESH
        )
        return carry

    def greet(i, carry):
        pl.semaphore_signal(
            barrier, inc=1, device_id=(lax.rem(me + i, n), half), device_id_type=MESH
        )
        return carry

    lax.fori_loop(1, m, greet_share, 0)
    lax.fori_loop(1, n, greet, 0)
    pl.semaphore_wait(barrier, m + n - 2)

    def started(make, stop):
        def run(i, carry):
            make(i).start()
            return carry
        lax.fori_loop(1, stop, run, 0)

    def waited(make, stop):
        def run(i, carry):
            make(i).wait()
            return carry
        lax.fori_loop(1, stop, run, 0)

    def share(i):
        to = lax.rem(half + i, m)
        return pltpu.make_async_remote_copy(
            src_ref=x.at[to], dst_ref=pair.at[i], send_sem=send0.at[i], recv_sem=recv0.at[i],
            device_id=(me, to), device_id_type=MESH,
        )

    started(share, m)
    waited(share, m)
    owned = lax.fori_loop(1, m, lambda i, total: total + pair[i], x[half])
    mine[...] = (owned * scaling).astype(jnp.bfloat16)

    def scatter(i):
        to = lax.rem(me + i, n)
        return pltpu.make_async_remote_copy(
            src_ref=mine.at[to], dst_ref=parts.at[i], send_sem=send1.at[i], recv_sem=recv1.at[i],
            device_id=(to, half), device_id_type=MESH,
        )

    def gather(i):
        return pltpu.make_async_remote_copy(
            src_ref=result.at[me], dst_ref=result.at[me], send_sem=send2.at[i],
            recv_sem=recv2.at[i], device_id=(lax.rem(me + i, n), half), device_id_type=MESH,
        )

    started(scatter, n)
    waited(scatter, n)

    def add(i, total):
        return total + parts[i].astype(jnp.float32)

    total = lax.fori_loop(1, n, add, mine[me].astype(jnp.float32))
    result[me] = total.astype(jnp.bfloat16)
    started(gather, n)
    waited(gather, n)
    out[...] = result[...].astype(jnp.float32)


def reduced(packed, scaling):
    m, n, rows, _ = packed.shape
    half = pltpu.VMEM((n, rows, LANES), jnp.bfloat16)
    return pl.pallas_call(
        functools.partial(reduce_kernel, m, n, scaling),
        in_specs=[pl.BlockSpec(memory_space=pltpu.VMEM)],
        out_specs=pl.BlockSpec(memory_space=pltpu.VMEM),
        out_shape=jax.ShapeDtypeStruct((n, rows, LANES), jnp.float32),
        scratch_shapes=[
            pltpu.VMEM((m, n, rows, LANES), jnp.float32),
            half,
            half,
            half,
            pltpu.SemaphoreType.DMA((m,)),
            pltpu.SemaphoreType.DMA((m,)),
            pltpu.SemaphoreType.DMA((n,)),
            pltpu.SemaphoreType.DMA((n,)),
            pltpu.SemaphoreType.DMA((n,)),
            pltpu.SemaphoreType.DMA((n,)),
        ],
        compiler_params=pltpu.CompilerParams(
            collective_id=0, has_side_effects=True, vmem_limit_bytes=32 << 20
        ),
        name="reduce",
    )(packed)


def body(proj, short_taps, long_filter, skip, grad_out, starts):
    source, upstream = proj[0], grad_out[0]
    tok, channels = upstream.shape
    count = lax.axis_size("ctx")
    pairs = lax.axis_size("fsdp")
    listed = jnp.pad(starts[0], ((0, 7), (0, LANES - starts.shape[2])), constant_values=tok)
    tail, taps, filt, factor, last, last_turned, row_turned = entry(
        pairs, count, source, short_taps, long_filter, skip[None], listed
    )
    ahead = filt[:, ::-1].transpose(0, 2, 1).reshape(-1, LEN)
    mixed, grads, low, edge, short, skip_part, lag = operate(
        count, last, last_turned, row_turned, factor, ahead, source, tail, taps, upstream
    )
    lag = lag.reshape(-1, LEN)
    returned = passed_along(edge[8 - (SHORT - 1) :].astype(jnp.bfloat16), "ctx", -1)
    fixed = low[8 - (SHORT - 1) :] + returned.astype(jnp.float32)
    grads = lax.dynamic_update_slice(grads, fixed.astype(jnp.bfloat16), (tok - (SHORT - 1), 0))

    scaling = float(pairs * count * tok) ** (-0.5)
    own = 3 * channels // pairs
    groups = channels // GROUP
    long_grad = lag[:, ::-1].T
    sizes = (SHORT * own, LEN * (groups // pairs), channels // pairs)
    flat = jnp.concatenate(
        [
            short.reshape(SHORT, pairs, own).transpose(1, 0, 2).reshape(pairs, -1),
            long_grad.reshape(LEN, pairs, groups // pairs).transpose(1, 0, 2).reshape(pairs, -1),
            skip_part.reshape(pairs, -1),
        ],
        axis=1,
    )
    unit = count * 16 * LANES
    padded = -(-flat.shape[1] // unit) * unit
    flat = jnp.pad(flat, ((0, 0), (0, padded - flat.shape[1])))
    summed = reduced(flat.reshape(pairs, count, -1, LANES), scaling).reshape(-1)
    a, b, c = sizes
    return (
        mixed[None],
        grads[None],
        summed[:a].reshape(SHORT, own),
        summed[a : a + b].reshape(LEN, groups // pairs),
        summed[a + b : a + b + c],
    )


def solution(mesh):
    window = P("fsdp", "ctx", None)
    return jax.shard_map(
        body,
        mesh=mesh,
        in_specs=(window, P(None, "fsdp"), P(None, "fsdp"), P("fsdp"), window, window),
        out_specs=(window, window, P(None, "fsdp"), P(None, "fsdp"), P("fsdp")),
        check_vma=False,
    )
```

```python
import functools

import jax
import jax.numpy as jnp
from jax import lax
from jax.experimental import pallas as pl
from jax.experimental.pallas import tpu as pltpu
from jax.sharding import PartitionSpec as P

GROUP = 16
LEN = 128
SHORT = 7
LANES = 128
FAR = 1 << 29
MESH = pl.DeviceIdType.MESH


def exchange_matrix(size):
    r = lax.broadcasted_iota(jnp.int32, (size, size), 0)
    c = lax.broadcasted_iota(jnp.int32, (size, size), 1)
    return (r + c == size - 1).astype(jnp.bfloat16)


def operator_kernel(
    m, n, per, scaling, proj, up, taps_own, filt_own, skip_own, starts,
    mixed, grads, out,
    taps, ahead, skip, tail, lists, last, last_turned, row_turned,
    feats, gate, glin, gate_prev, glin_next, pad, spill, tiles_f, tiles_b, picked,
    weights, low, edge, edge_out, edge_in, pair, mine, parts, result,
    gate_send, gate_recv, glin_send, glin_recv, near_send, near_recv, share_send, share_recv,
    send0, recv0, send1, recv1, send2, recv2,
):
    me, half = lax.axis_index("ctx"), lax.axis_index("fsdp")
    right, left = lax.rem(me + 1, n), lax.rem(me + n - 1, n)
    blocks, tok = gate.shape[0], gate.shape[1]
    chunks, count = blocks // per, LANES // GROUP
    f32, bf16 = jnp.float32, jnp.bfloat16
    barrier = pltpu.get_barrier_semaphore()

    def greet_share(i, carry):
        pl.semaphore_signal(
            barrier, inc=1, device_id=(me, lax.rem(half + i, m)), device_id_type=MESH
        )
        return carry

    def greet(i, carry):
        pl.semaphore_signal(
            barrier, inc=1, device_id=(lax.rem(me + i, n), half), device_id_type=MESH
        )
        return carry

    lax.fori_loop(1, m, greet_share, 0)
    lax.fori_loop(1, n, greet, 0)
    pl.semaphore_wait(barrier, m + n - 2)

    def started(make, stop, first=1):
        def run(i, carry):
            make(i).start()
            return carry
        lax.fori_loop(first, stop, run, 0)

    def waited(make, stop, first=1):
        def run(i, carry):
            make(i).wait()
            return carry
        lax.fori_loop(first, stop, run, 0)

    def near(j, src, dst, to):
        return pltpu.make_async_remote_copy(
            src_ref=src, dst_ref=dst, send_sem=near_send.at[j], recv_sem=near_recv.at[j],
            device_id=(to, half), device_id_type=MESH,
        )

    entry = [
        near(0, proj.at[tok - 16 : tok], tail, right),
        near(1, starts, lists.at[0], right),
        near(2, starts, lists.at[2], left),
    ]
    for copy in entry:
        copy.start()
    width, skips, groups = taps_own.shape[1], skip_own.shape[1], filt_own.shape[0]
    taps_at = pl.ds(pl.multiple_of(half * width, LANES), width)
    skip_at = pl.ds(pl.multiple_of(half * skips, LANES), skips)
    filt_at = pl.ds(pl.multiple_of(half * groups, 8), groups)

    def shares(j):
        src, dst = (
            (taps_own, taps.at[:, taps_at]),
            (filt_own, ahead.at[filt_at]),
            (skip_own, skip.at[:, skip_at]),
        )[j]

        def make(i):
            return pltpu.make_async_remote_copy(
                src_ref=src, dst_ref=dst, send_sem=share_send.at[j, i],
                recv_sem=share_recv.at[j, i], device_id=(me, lax.rem(half + i, m)),
                device_id_type=MESH,
            )
        return make

    for j in range(3):
        started(shares(j), m)
    lists[1] = starts[...]
    taps[:, taps_at] = taps_own[...]
    ahead[filt_at] = filt_own[...]
    skip[:, skip_at] = skip_own[...]
    weights[...] = jnp.zeros(weights.shape, f32)
    rows = lax.broadcasted_iota(jnp.int32, (tok, LANES), 0)
    cols = lax.broadcasted_iota(jnp.int32, (tok, LANES), 1)
    for copy in entry:
        copy.wait()

    def latest(places):
        best = jnp.full((tok, LANES), -FAR, jnp.int32)
        for j in range(3):
            listed = lists[j, 0:1, :]
            placed = jnp.where(listed < tok, listed + (j - 1) * tok, -FAR)
            best = jnp.maximum(best, jnp.where(placed <= places, placed, -FAR))
        top = jnp.max(best.astype(f32), axis=1, keepdims=True)
        return jnp.broadcast_to(top, (tok, LANES))

    def as_row(column):
        row = jnp.sum(jnp.where(rows == cols, column, 0.0), axis=0, keepdims=True)
        return jnp.broadcast_to(row.astype(jnp.int32), (8, tok))

    turned_last = latest(tok - 1 - rows)
    last[...] = latest(rows).astype(jnp.int32)
    last_turned[...] = turned_last.astype(jnp.int32)
    later = as_row(latest(2 * tok - 1 - rows))
    row_turned[:, :tok] = jnp.where(me < n - 1, later, FAR)
    row_turned[:, tok:] = as_row(turned_last)
    for j in range(3):
        waited(shares(j), m)
    spill[:, 0:8, :] = jnp.zeros((SHORT, 8, LANES), f32)
    spill[:, tok + 8 :, :] = jnp.zeros((SHORT, 8, LANES), f32)

    def lanes(block, part=0):
        return pl.ds(pl.multiple_of((part * blocks + block) * LANES, LANES), LANES)

    def copies(chunk):
        at = pl.ds(chunk * per, per)
        return (
            pltpu.make_async_remote_copy(
                src_ref=gate.at[at], dst_ref=gate_prev.at[at], send_sem=gate_send.at[chunk],
                recv_sem=gate_recv.at[chunk], device_id=(right, half), device_id_type=MESH,
            ),
            pltpu.make_async_remote_copy(
                src_ref=glin.at[at], dst_ref=glin_next.at[at], send_sem=glin_send.at[chunk],
                recv_sem=glin_recv.at[chunk], device_id=(left, half), device_id_type=MESH,
            ),
        )

    def load_rows(block):
        for part in range(3):
            at = lanes(block, part)
            pad[part, 0:8, :] = tail[:, at].astype(f32)[8:16]
            pad[part, 8:, :] = proj[:, at].astype(f32)

    def earlier(part, offset):
        return pad[part, 8 - offset : 8 - offset + tok, :]

    def featurize(block, carry):
        load_rows(block)
        made = []
        for part in range(3):
            at = lanes(block, part)
            total = jnp.zeros((tok, LANES), f32)
            for offset in range(SHORT):
                kept = jnp.where(last[...] <= rows - offset, earlier(part, offset), 0.0)
                total = total + taps[offset : offset + 1, at] * kept
            feats[part, block] = total
            made.append(total)
        gate[block] = (made[1] * made[2]).astype(bf16)
        through = (up[:, lanes(block)].astype(f32) * made[0]).astype(bf16)
        turned = jnp.dot(exchange_matrix(tok), through, preferred_element_type=f32)
        glin[block] = turned.astype(bf16)
        return carry

    def prepare(chunk, carry):
        lax.fori_loop(chunk * per, (chunk + 1) * per, featurize, 0)
        for copy in copies(chunk):
            copy.start()
        return carry

    lax.fori_loop(0, chunks, prepare, 0)

    kept_blocks = blocks // m

    def convolve(block, carry):
        at = lanes(block)
        lag_half, lag_at = block // kept_blocks, 3 * kept_blocks + lax.rem(block, kept_blocks)
        start = last[...]
        start_turned = last_turned[...]
        below = cols <= rows
        fwd_prev = jnp.logical_and(cols > rows, start <= cols - tok)
        fwd_own = jnp.logical_and(below, start <= cols)
        turned = tok - 1 - rows
        bwd_next = jnp.logical_and(cols > rows, row_turned[0:1, :tok] <= turned)
        bwd_own = jnp.logical_and(below, row_turned[0:1, tok:] <= turned)
        lag_prev = jnp.logical_and(cols > turned, start_turned <= cols - tok)
        lag_own = jnp.logical_and(cols <= turned, start_turned <= cols)
        lane = cols // GROUP
        own_gate, own_glin = gate[block], glin[block]
        gate_win = jnp.concatenate([gate_prev[block], own_gate], axis=0)
        glin_win = jnp.concatenate([glin_next[block], own_glin], axis=0)
        glin_f = own_glin.astype(f32)
        filters = ahead[pl.ds(pl.multiple_of(block * count, count), count), :]
        for g in range(count):
            part = slice(g * tok, (g + 1) * tok)
            tile = jnp.broadcast_to(filters[g : g + 1, :], (tok, LEN))
            tile = pltpu.roll(tile, 1, 1, stride=1, stride_axis=0)
            tiles_f[part, :tok] = jnp.where(fwd_prev, tile, 0.0).astype(bf16)
            tiles_f[part, tok:] = jnp.where(fwd_own, tile, 0.0).astype(bf16)
            tiles_b[part, :tok] = jnp.where(bwd_next, tile, 0.0).astype(bf16)
            tiles_b[part, tok:] = jnp.where(bwd_own, tile, 0.0).astype(bf16)
            picked[part, :] = jnp.where(lane == g, glin_f, 0.0).astype(bf16)
        out_f = jnp.dot(tiles_f[...], gate_win, preferred_element_type=f32)
        out_b = jnp.dot(tiles_b[...], glin_win, preferred_element_type=f32)
        product = lax.dot_general(
            picked[...], gate_win, (((1,), (1,)), ((), ())), preferred_element_type=f32
        )
        long_out, spread = out_f[:tok], out_b[:tok]
        for g in range(count):
            part = slice(g * tok, (g + 1) * tok)
            if g:
                long_out = jnp.where(lane == g, out_f[part], long_out)
                spread = jnp.where(lane == g, out_b[part], spread)
            folded = jnp.where(lag_prev, product[part, :tok], 0.0)
            folded = jnp.where(lag_own, product[part, tok:], folded)
            folded = pltpu.roll(folded, 0, 1, stride=1, stride_axis=0)
            weights[lag_half, lag_at, g : g + 1, :] = jnp.sum(folded, axis=0, keepdims=True)
        flip = exchange_matrix(tok)
        high = spread.astype(bf16)
        rest = (spread - high.astype(f32)).astype(bf16)
        spread = jnp.dot(flip, high, preferred_element_type=f32) + jnp.dot(
            flip, rest, preferred_element_type=f32
        )
        gate_f = own_gate.astype(f32)
        query, key, value = feats[0, block], feats[1, block], feats[2, block]
        upstream = up[:, at].astype(f32)
        factor = skip[:, at]
        combined = long_out + factor * gate_f
        mixed[:, at] = (query * combined).astype(bf16)
        through = upstream * query
        weights[lag_half, lax.rem(block, kept_blocks), SHORT : SHORT + 1, :] = jnp.sum(
            through * gate_f, axis=0, keepdims=True
        )
        grad_gate = spread + factor * through
        load_rows(block)
        for part, grad in enumerate((upstream * combined, grad_gate * value, grad_gate * key)):
            at = lanes(block, part)
            column = part * blocks + block
            owner, place = column // (3 * kept_blocks), lax.rem(column, 3 * kept_blocks)
            for offset in range(SHORT):
                kept = jnp.where(start <= rows - offset, grad, 0.0)
                weights[owner, place, offset : offset + 1, :] = jnp.sum(
                    kept * earlier(part, offset), axis=0, keepdims=True
                )
                spill[offset, 8 : tok + 8, :] = taps[offset : offset + 1, at] * kept
            total = spill[0, 0 : tok + 8, :]
            for offset in range(1, SHORT):
                total = total + spill[offset, offset : offset + tok + 8, :]
            grads[:, at] = total[8:].astype(bf16)
            low[column] = total[tok - 8 :]
            edge[column] = total[:8]
        return carry

    def use(chunk, carry):
        for copy in copies(chunk):
            copy.wait_recv()
        lax.fori_loop(chunk * per, (chunk + 1) * per, convolve, 0)
        return carry

    lax.fori_loop(0, chunks, use, 0)

    def sent(chunk, carry):
        for copy in copies(chunk):
            copy.wait_send()
        return carry

    lax.fori_loop(0, chunks, sent, 0)
    edge_out[...] = edge[...].reshape(edge_out.shape).astype(bf16)
    back = near(3, edge_out, edge_in, left)
    back.start()

    def share(i):
        to = lax.rem(half + i, m)
        return pltpu.make_async_remote_copy(
            src_ref=weights.at[to], dst_ref=pair.at[i], send_sem=send0.at[i],
            recv_sem=recv0.at[i], device_id=(me, to), device_id_type=MESH,
        )

    def scatter(i):
        to = lax.rem(me + i, n)
        return pltpu.make_async_remote_copy(
            src_ref=mine.at[to], dst_ref=parts.at[i], send_sem=send1.at[i], recv_sem=recv1.at[i],
            device_id=(to, half), device_id_type=MESH,
        )

    def gather(i):
        return pltpu.make_async_remote_copy(
            src_ref=result.at[me], dst_ref=result.at[me], send_sem=send2.at[i],
            recv_sem=recv2.at[i], device_id=(lax.rem(me + i, n), half), device_id_type=MESH,
        )

    started(share, m)
    waited(share, m)
    owned = lax.fori_loop(1, m, lambda i, total: total + pair[i], weights[half])
    mine[...] = (owned * scaling).reshape(mine.shape).astype(bf16)
    started(scatter, n)
    back.wait()
    edge[...] = edge_in[...].astype(f32).reshape(edge.shape)

    def mend(column, carry):
        at = pl.ds(pl.multiple_of(column * LANES, LANES), LANES)
        total = jnp.concatenate([low[column, :8], low[column, 8:] + edge[column]], axis=0)
        grads[tok - 16 :, at] = total.astype(bf16)
        return carry

    lax.fori_loop(0, 3 * blocks, mend, 0)
    waited(scatter, n)

    def add(i, total):
        return total + parts[i].astype(f32)

    total = lax.fori_loop(1, n, add, mine[me].astype(f32))
    result[me] = total.astype(bf16)
    started(gather, n)
    waited(gather, n)
    out[...] = result[...].astype(f32).reshape(out.shape)


def operate(m, n, scaling, source, upstream, taps, filt, skip, starts):
    tok, channels = upstream.shape
    blocks = channels // LANES
    per = min(4, blocks)
    count = LANES // GROUP
    units = -(-4 * (blocks // m) // n)
    units += units % 2
    f32, bf16, i32 = jnp.float32, jnp.bfloat16, jnp.int32
    vmem = pl.BlockSpec(memory_space=pltpu.VMEM)
    half = pltpu.VMEM((blocks, tok, LANES), bf16)
    tiles = pltpu.VMEM((count * tok, 2 * tok), bf16)
    sems = pltpu.SemaphoreType.DMA((blocks // per,))
    edges = pltpu.VMEM((3 * blocks // 2, 16, LANES), bf16)
    share = pltpu.VMEM((m, n * units, 8, LANES), f32)
    sums = pltpu.VMEM((n, 8 * units, LANES), bf16)
    return pl.pallas_call(
        functools.partial(operator_kernel, m, n, per, scaling),
        in_specs=[vmem] * 6,
        out_specs=[vmem] * 3,
        out_shape=[
            jax.ShapeDtypeStruct((tok, channels), bf16),
            jax.ShapeDtypeStruct((tok, 3 * channels), bf16),
            jax.ShapeDtypeStruct((n * units, 8, LANES), f32),
        ],
        scratch_shapes=[
            pltpu.VMEM((SHORT, 3 * channels), f32),
            pltpu.VMEM((channels // GROUP, LEN), f32),
            pltpu.VMEM((1, channels), f32),
            pltpu.VMEM((16, 3 * channels), bf16),
            pltpu.VMEM((3, 8, LANES), i32),
            pltpu.VMEM((tok, LANES), i32),
            pltpu.VMEM((tok, LANES), i32),
            pltpu.VMEM((8, 2 * tok), i32),
            pltpu.VMEM((3, blocks, tok, LANES), f32),
            half,
            half,
            half,
            half,
            pltpu.VMEM((3, tok + 8, LANES), f32),
            pltpu.VMEM((SHORT, tok + 16, LANES), f32),
            tiles,
            tiles,
            pltpu.VMEM((count * tok, LANES), bf16),
            share,
            pltpu.VMEM((3 * blocks, 16, LANES), f32),
            pltpu.VMEM((3 * blocks, 8, LANES), f32),
            edges,
            edges,
            share,
            sums,
            sums,
            sums,
            sems,
            sems,
            sems,
            sems,
            pltpu.SemaphoreType.DMA((4,)),
            pltpu.SemaphoreType.DMA((4,)),
            pltpu.SemaphoreType.DMA((3, m)),
            pltpu.SemaphoreType.DMA((3, m)),
            pltpu.SemaphoreType.DMA((m,)),
            pltpu.SemaphoreType.DMA((m,)),
            pltpu.SemaphoreType.DMA((n,)),
            pltpu.SemaphoreType.DMA((n,)),
            pltpu.SemaphoreType.DMA((n,)),
            pltpu.SemaphoreType.DMA((n,)),
        ],
        compiler_params=pltpu.CompilerParams(
            collective_id=0, has_side_effects=True, vmem_limit_bytes=50 << 20
        ),
        name="operate",
    )(source, upstream, taps, filt, skip, starts)


def body(proj, short_taps, long_filter, skip, grad_out, starts):
    source, upstream = proj[0], grad_out[0]
    tok, channels = upstream.shape
    count, pairs = lax.axis_size("ctx"), lax.axis_size("fsdp")
    scaling = float(pairs * count * tok) ** (-0.5)
    listed = jnp.pad(starts[0], ((0, 7), (0, LANES - starts.shape[2])), constant_values=tok)
    mixed, grads, sums = operate(
        pairs, count, scaling, source, upstream, short_taps, long_filter[::-1].T, skip[None], listed
    )
    kept = channels // LANES // pairs
    return (
        mixed[None],
        grads[None],
        sums[: 3 * kept, :SHORT].transpose(1, 0, 2).reshape(SHORT, -1),
        sums[3 * kept : 4 * kept].reshape(-1, LEN)[:, ::-1].T,
        sums[:kept, SHORT].reshape(-1),
    )


def solution(mesh):
    window = P("fsdp", "ctx", None)
    return jax.shard_map(
        body,
        mesh=mesh,
        in_specs=(window, P(None, "fsdp"), P(None, "fsdp"), P("fsdp"), window, window),
        out_specs=(window, window, P(None, "fsdp"), P(None, "fsdp"), P("fsdp")),
        check_vma=False,
    )
```

```python
import functools

import jax
import jax.numpy as jnp
from jax import lax
from jax.experimental import pallas as pl
from jax.experimental.pallas import tpu as pltpu
from jax.sharding import PartitionSpec as P

GROUP = 16
LEN = 128
SHORT = 7
LANES = 128
FAR = 1 << 29
MESH = pl.DeviceIdType.MESH


def exchange_matrix(size):
    r = lax.broadcasted_iota(jnp.int32, (size, size), 0)
    c = lax.broadcasted_iota(jnp.int32, (size, size), 1)
    return (r + c == size - 1).astype(jnp.bfloat16)


def operator_kernel(
    m, n, per, scaling, proj, up, taps_own, filt_own, skip_own, starts,
    mixed, grads, out,
    taps, ahead, skip, tail, lists, last, last_turned, row_turned,
    feats, gate, glin, gate_prev, glin_next, pad, spill, tiles_f, tiles_b, picked,
    weights, low, edge, edge_out, edge_in, pair, mine, parts, result,
    gate_send, gate_recv, glin_send, glin_recv, near_send, near_recv, share_send, share_recv,
    send0, recv0, send1, recv1, send2, recv2,
):
    me, half = lax.axis_index("ctx"), lax.axis_index("fsdp")
    right, left = lax.rem(me + 1, n), lax.rem(me + n - 1, n)
    blocks, tok = gate.shape[0], gate.shape[1]
    chunks, count = blocks // per, LANES // GROUP
    f32, bf16 = jnp.float32, jnp.bfloat16
    barrier = pltpu.get_barrier_semaphore()

    def greet_share(i, carry):
        pl.semaphore_signal(
            barrier, inc=1, device_id=(me, lax.rem(half + i, m)), device_id_type=MESH
        )
        return carry

    def greet(i, carry):
        pl.semaphore_signal(
            barrier, inc=1, device_id=(lax.rem(me + i, n), half), device_id_type=MESH
        )
        return carry

    lax.fori_loop(1, m, greet_share, 0)
    lax.fori_loop(1, n, greet, 0)
    pl.semaphore_wait(barrier, m + n - 2)

    def started(make, stop, first=1):
        def run(i, carry):
            make(i).start()
            return carry
        lax.fori_loop(first, stop, run, 0)

    def waited(make, stop, first=1):
        def run(i, carry):
            make(i).wait()
            return carry
        lax.fori_loop(first, stop, run, 0)

    def near(j, src, dst, to):
        return pltpu.make_async_remote_copy(
            src_ref=src, dst_ref=dst, send_sem=near_send.at[j], recv_sem=near_recv.at[j],
            device_id=(to, half), device_id_type=MESH,
        )

    entry = [
        near(0, proj.at[tok - 16 : tok], tail, right),
        near(1, starts, lists.at[0], right),
        near(2, starts, lists.at[2], left),
    ]
    for copy in entry:
        copy.start()
    width, skips, groups = taps_own.shape[1], skip_own.shape[1], filt_own.shape[0]
    taps_at = pl.ds(pl.multiple_of(half * width, LANES), width)
    skip_at = pl.ds(pl.multiple_of(half * skips, LANES), skips)
    filt_at = pl.ds(pl.multiple_of(half * groups, 8), groups)

    def shares(j):
        src, dst = (
            (taps_own, taps.at[:, taps_at]),
            (filt_own, ahead.at[filt_at]),
            (skip_own, skip.at[:, skip_at]),
        )[j]

        def make(i):
            return pltpu.make_async_remote_copy(
                src_ref=src, dst_ref=dst, send_sem=share_send.at[j, i],
                recv_sem=share_recv.at[j, i], device_id=(me, lax.rem(half + i, m)),
                device_id_type=MESH,
            )
        return make

    for j in range(3):
        started(shares(j), m)
    lists[1] = starts[...]
    taps[:, taps_at] = taps_own[...]
    ahead[filt_at] = filt_own[...]
    skip[:, skip_at] = skip_own[...]
    weights[...] = jnp.zeros(weights.shape, f32)
    rows = lax.broadcasted_iota(jnp.int32, (tok, LANES), 0)
    cols = lax.broadcasted_iota(jnp.int32, (tok, LANES), 1)
    for copy in entry:
        copy.wait()

    def latest(places):
        best = jnp.full((tok, LANES), -FAR, jnp.int32)
        for j in range(3):
            listed = lists[j, 0:1, :]
            placed = jnp.where(listed < tok, listed + (j - 1) * tok, -FAR)
            best = jnp.maximum(best, jnp.where(placed <= places, placed, -FAR))
        top = jnp.max(best.astype(f32), axis=1, keepdims=True)
        return jnp.broadcast_to(top, (tok, LANES))

    def as_row(column):
        row = jnp.sum(jnp.where(rows == cols, column, 0.0), axis=0, keepdims=True)
        return jnp.broadcast_to(row.astype(jnp.int32), (8, tok))

    turned_last = latest(tok - 1 - rows)
    last[...] = latest(rows).astype(jnp.int32)
    last_turned[...] = turned_last.astype(jnp.int32)
    later = as_row(latest(2 * tok - 1 - rows))
    row_turned[:, :tok] = jnp.where(me < n - 1, later, FAR)
    row_turned[:, tok:] = as_row(turned_last)
    for j in range(3):
        waited(shares(j), m)
    spill[:, :, 0:8, :] = jnp.zeros((2, SHORT, 8, LANES), f32)
    spill[:, :, tok + 8 :, :] = jnp.zeros((2, SHORT, 8, LANES), f32)

    def lanes(block, part=0):
        return pl.ds(pl.multiple_of((part * blocks + block) * LANES, LANES), LANES)

    def copies(chunk):
        at = pl.ds(chunk * per, per)
        return (
            pltpu.make_async_remote_copy(
                src_ref=gate.at[at], dst_ref=gate_prev.at[at], send_sem=gate_send.at[chunk],
                recv_sem=gate_recv.at[chunk], device_id=(right, half), device_id_type=MESH,
            ),
            pltpu.make_async_remote_copy(
                src_ref=glin.at[at], dst_ref=glin_next.at[at], send_sem=glin_send.at[chunk],
                recv_sem=glin_recv.at[chunk], device_id=(left, half), device_id_type=MESH,
            ),
        )

    def load_rows(block, slot=0):
        for part in range(3):
            at = lanes(block, part)
            pad[slot, part, 0:8, :] = tail[:, at].astype(f32)[8:16]
            pad[slot, part, 8:, :] = proj[:, at].astype(f32)

    def earlier(part, offset, slot=0):
        return pad[slot, part, 8 - offset : 8 - offset + tok, :]

    def featurize(block, carry):
        load_rows(block)
        made = []
        for part in range(3):
            at = lanes(block, part)
            total = jnp.zeros((tok, LANES), f32)
            for offset in range(SHORT):
                kept = jnp.where(last[...] <= rows - offset, earlier(part, offset), 0.0)
                total = total + taps[offset : offset + 1, at] * kept
            feats[part, block] = total
            made.append(total)
        gate[block] = (made[1] * made[2]).astype(bf16)
        through = (up[:, lanes(block)].astype(f32) * made[0]).astype(bf16)
        turned = jnp.dot(exchange_matrix(tok), through, preferred_element_type=f32)
        glin[block] = turned.astype(bf16)
        return carry

    def prepare(chunk, carry):
        lax.fori_loop(chunk * per, (chunk + 1) * per, featurize, 0)
        for copy in copies(chunk):
            copy.start()
        return carry

    lax.fori_loop(0, chunks, prepare, 0)

    kept_blocks = blocks // m

    def convolve(block, slot):
        at = lanes(block)
        lag_half, lag_at = block // kept_blocks, 3 * kept_blocks + lax.rem(block, kept_blocks)
        start = last[...]
        start_turned = last_turned[...]
        below = cols <= rows
        fwd_prev = jnp.logical_and(cols > rows, start <= cols - tok)
        fwd_own = jnp.logical_and(below, start <= cols)
        turned = tok - 1 - rows
        bwd_next = jnp.logical_and(cols > rows, row_turned[0:1, :tok] <= turned)
        bwd_own = jnp.logical_and(below, row_turned[0:1, tok:] <= turned)
        lag_prev = jnp.logical_and(cols > turned, start_turned <= cols - tok)
        lag_own = jnp.logical_and(cols <= turned, start_turned <= cols)
        lane = cols // GROUP
        own_gate, own_glin = gate[block], glin[block]
        gate_win = jnp.concatenate([gate_prev[block], own_gate], axis=0)
        glin_win = jnp.concatenate([glin_next[block], own_glin], axis=0)
        glin_f = own_glin.astype(f32)
        filters = ahead[pl.ds(pl.multiple_of(block * count, count), count), :]
        for g in range(count):
            part = slice(g * tok, (g + 1) * tok)
            tile = jnp.broadcast_to(filters[g : g + 1, :], (tok, LEN))
            tile = pltpu.roll(tile, 1, 1, stride=1, stride_axis=0)
            tiles_f[slot, part, :tok] = jnp.where(fwd_prev, tile, 0.0).astype(bf16)
            tiles_f[slot, part, tok:] = jnp.where(fwd_own, tile, 0.0).astype(bf16)
            tiles_b[slot, part, :tok] = jnp.where(bwd_next, tile, 0.0).astype(bf16)
            tiles_b[slot, part, tok:] = jnp.where(bwd_own, tile, 0.0).astype(bf16)
            picked[slot, part, :] = jnp.where(lane == g, glin_f, 0.0).astype(bf16)
        out_f = jnp.dot(tiles_f[slot], gate_win, preferred_element_type=f32)
        out_b = jnp.dot(tiles_b[slot], glin_win, preferred_element_type=f32)
        product = lax.dot_general(
            picked[slot], gate_win, (((1,), (1,)), ((), ())), preferred_element_type=f32
        )
        long_out, spread = out_f[:tok], out_b[:tok]
        for g in range(count):
            part = slice(g * tok, (g + 1) * tok)
            if g:
                long_out = jnp.where(lane == g, out_f[part], long_out)
                spread = jnp.where(lane == g, out_b[part], spread)
            folded = jnp.where(lag_prev, product[part, :tok], 0.0)
            folded = jnp.where(lag_own, product[part, tok:], folded)
            folded = pltpu.roll(folded, 0, 1, stride=1, stride_axis=0)
            weights[lag_half, lag_at, g : g + 1, :] = jnp.sum(folded, axis=0, keepdims=True)
        flip = exchange_matrix(tok)
        high = spread.astype(bf16)
        rest = (spread - high.astype(f32)).astype(bf16)
        spread = jnp.dot(flip, high, preferred_element_type=f32) + jnp.dot(
            flip, rest, preferred_element_type=f32
        )
        gate_f = own_gate.astype(f32)
        query, key, value = feats[0, block], feats[1, block], feats[2, block]
        upstream = up[:, at].astype(f32)
        factor = skip[:, at]
        combined = long_out + factor * gate_f
        mixed[:, at] = (query * combined).astype(bf16)
        through = upstream * query
        weights[lag_half, lax.rem(block, kept_blocks), SHORT : SHORT + 1, :] = jnp.sum(
            through * gate_f, axis=0, keepdims=True
        )
        grad_gate = spread + factor * through
        load_rows(block, slot)
        for part, grad in enumerate((upstream * combined, grad_gate * value, grad_gate * key)):
            at = lanes(block, part)
            column = part * blocks + block
            owner, place = column // (3 * kept_blocks), lax.rem(column, 3 * kept_blocks)
            for offset in range(SHORT):
                kept = jnp.where(start <= rows - offset, grad, 0.0)
                weights[owner, place, offset : offset + 1, :] = jnp.sum(
                    kept * earlier(part, offset, slot), axis=0, keepdims=True
                )
                spill[slot, offset, 8 : tok + 8, :] = taps[offset : offset + 1, at] * kept
            total = spill[slot, 0, 0 : tok + 8, :]
            for offset in range(1, SHORT):
                total = total + spill[slot, offset, offset : offset + tok + 8, :]
            grads[:, at] = total[8:].astype(bf16)
            low[column] = total[tok - 8 :]
            edge[column] = total[:8]

    def both(pair_at, carry):
        convolve(2 * pair_at, 0)
        convolve(2 * pair_at + 1, 1)
        return carry

    def use(chunk, carry):
        for copy in copies(chunk):
            copy.wait_recv()
        lax.fori_loop(chunk * (per // 2), (chunk + 1) * (per // 2), both, 0)
        return carry

    lax.fori_loop(0, chunks, use, 0)

    def sent(chunk, carry):
        for copy in copies(chunk):
            copy.wait_send()
        return carry

    lax.fori_loop(0, chunks, sent, 0)
    edge_out[...] = edge[...].reshape(edge_out.shape).astype(bf16)
    back = near(3, edge_out, edge_in, left)
    back.start()

    def share(i):
        to = lax.rem(half + i, m)
        return pltpu.make_async_remote_copy(
            src_ref=weights.at[to], dst_ref=pair.at[i], send_sem=send0.at[i],
            recv_sem=recv0.at[i], device_id=(me, to), device_id_type=MESH,
        )

    def scatter(i):
        to = lax.rem(me + i, n)
        return pltpu.make_async_remote_copy(
            src_ref=mine.at[to], dst_ref=parts.at[i], send_sem=send1.at[i], recv_sem=recv1.at[i],
            device_id=(to, half), device_id_type=MESH,
        )

    def gather(i):
        return pltpu.make_async_remote_copy(
            src_ref=result.at[me], dst_ref=result.at[me], send_sem=send2.at[i],
            recv_sem=recv2.at[i], device_id=(lax.rem(me + i, n), half), device_id_type=MESH,
        )

    started(share, m)
    waited(share, m)
    owned = lax.fori_loop(1, m, lambda i, total: total + pair[i], weights[half])
    mine[...] = (owned * scaling).reshape(mine.shape).astype(bf16)
    started(scatter, n)
    back.wait()
    edge[...] = edge_in[...].astype(f32).reshape(edge.shape)

    def mend(column, carry):
        at = pl.ds(pl.multiple_of(column * LANES, LANES), LANES)
        total = jnp.concatenate([low[column, :8], low[column, 8:] + edge[column]], axis=0)
        grads[tok - 16 :, at] = total.astype(bf16)
        return carry

    lax.fori_loop(0, 3 * blocks, mend, 0)
    waited(scatter, n)

    def add(i, total):
        return total + parts[i].astype(f32)

    total = lax.fori_loop(1, n, add, mine[me].astype(f32))
    result[me] = total.astype(bf16)
    started(gather, n)
    waited(gather, n)
    out[...] = result[...].astype(f32).reshape(out.shape)


def operate(m, n, scaling, source, upstream, taps, filt, skip, starts):
    tok, channels = upstream.shape
    blocks = channels // LANES
    per = min(4, blocks)
    count = LANES // GROUP
    units = -(-4 * (blocks // m) // n)
    units += units % 2
    f32, bf16, i32 = jnp.float32, jnp.bfloat16, jnp.int32
    vmem = pl.BlockSpec(memory_space=pltpu.VMEM)
    half = pltpu.VMEM((blocks, tok, LANES), bf16)
    tiles = pltpu.VMEM((2, count * tok, 2 * tok), bf16)
    sems = pltpu.SemaphoreType.DMA((blocks // per,))
    edges = pltpu.VMEM((3 * blocks // 2, 16, LANES), bf16)
    share = pltpu.VMEM((m, n * units, 8, LANES), f32)
    sums = pltpu.VMEM((n, 8 * units, LANES), bf16)
    return pl.pallas_call(
        functools.partial(operator_kernel, m, n, per, scaling),
        in_specs=[vmem] * 6,
        out_specs=[vmem] * 3,
        out_shape=[
            jax.ShapeDtypeStruct((tok, channels), bf16),
            jax.ShapeDtypeStruct((tok, 3 * channels), bf16),
            jax.ShapeDtypeStruct((n * units, 8, LANES), f32),
        ],
        scratch_shapes=[
            pltpu.VMEM((SHORT, 3 * channels), f32),
            pltpu.VMEM((channels // GROUP, LEN), f32),
            pltpu.VMEM((1, channels), f32),
            pltpu.VMEM((16, 3 * channels), bf16),
            pltpu.VMEM((3, 8, LANES), i32),
            pltpu.VMEM((tok, LANES), i32),
            pltpu.VMEM((tok, LANES), i32),
            pltpu.VMEM((8, 2 * tok), i32),
            pltpu.VMEM((3, blocks, tok, LANES), f32),
            half,
            half,
            half,
            half,
            pltpu.VMEM((2, 3, tok + 8, LANES), f32),
            pltpu.VMEM((2, SHORT, tok + 16, LANES), f32),
            tiles,
            tiles,
            pltpu.VMEM((2, count * tok, LANES), bf16),
            share,
            pltpu.VMEM((3 * blocks, 16, LANES), f32),
            pltpu.VMEM((3 * blocks, 8, LANES), f32),
            edges,
            edges,
            share,
            sums,
            sums,
            sums,
            sems,
            sems,
            sems,
            sems,
            pltpu.SemaphoreType.DMA((4,)),
            pltpu.SemaphoreType.DMA((4,)),
            pltpu.SemaphoreType.DMA((3, m)),
            pltpu.SemaphoreType.DMA((3, m)),
            pltpu.SemaphoreType.DMA((m,)),
            pltpu.SemaphoreType.DMA((m,)),
            pltpu.SemaphoreType.DMA((n,)),
            pltpu.SemaphoreType.DMA((n,)),
            pltpu.SemaphoreType.DMA((n,)),
            pltpu.SemaphoreType.DMA((n,)),
        ],
        compiler_params=pltpu.CompilerParams(
            collective_id=0, has_side_effects=True, vmem_limit_bytes=50 << 20
        ),
        name="operate",
    )(source, upstream, taps, filt, skip, starts)


def body(proj, short_taps, long_filter, skip, grad_out, starts):
    source, upstream = proj[0], grad_out[0]
    tok, channels = upstream.shape
    count, pairs = lax.axis_size("ctx"), lax.axis_size("fsdp")
    scaling = float(pairs * count * tok) ** (-0.5)
    listed = jnp.pad(starts[0], ((0, 7), (0, LANES - starts.shape[2])), constant_values=tok)
    mixed, grads, sums = operate(
        pairs, count, scaling, source, upstream, short_taps, long_filter[::-1].T, skip[None], listed
    )
    kept = channels // LANES // pairs
    return (
        mixed[None],
        grads[None],
        sums[: 3 * kept, :SHORT].transpose(1, 0, 2).reshape(SHORT, -1),
        sums[3 * kept : 4 * kept].reshape(-1, LEN)[:, ::-1].T,
        sums[:kept, SHORT].reshape(-1),
    )


def solution(mesh):
    window = P("fsdp", "ctx", None)
    return jax.shard_map(
        body,
        mesh=mesh,
        in_specs=(window, P(None, "fsdp"), P(None, "fsdp"), P("fsdp"), window, window),
        out_specs=(window, window, P(None, "fsdp"), P(None, "fsdp"), P("fsdp")),
        check_vma=False,
    )
```
